32 devices in a mesh: group: 2 (over x), mod: 4 (over y, core), dir: 4 (over z).
Axes of the slice: x: 2, y: 2, z: 4, core: 2. Of those that a mesh axis runs over, the one named last changes fastest.
Arguments:
- screens: float32 [8, 512, 512], P('group', 'mod'), parts along dimension 0, may hold values from -6 to 6
- footprint: int32 [8, 4, 2], P(('group', 'dir')), parts along dimension 0, may hold values from 0 to 191
- fraction: int32 [8, 4, 2], P(('group', 'dir')), parts along dimension 0, may hold values from 0 to 15
- tilt_steps: int32 [16, 2], P(('group', 'mod')), parts along dimension 0, may hold values from -64 to 64
- facet_shift: int32 [4, 2], replicated, may hold values from 80 to 160
Outputs:
- detector: float32 [8, 640, 640], P(('group', 'dir'), 'mod'), parts along dimension 0
The draws below stay inside these ranges and needn't reach their ends.
There are 2 independent parts, one for each index of `group`. The reference program is written for one: setup_inputs(seed, part) draws one part's arguments, and reference() takes and returns one part's arrays. A program takes and returns all parts, laid end to end along the dimension named above; an argument that names none is the same for every part. Nothing has to cross between parts.
All inputs are finite; a program needn't handle non-finite values.
Results may differ from the reference program's by a relative error of at most 0.0055.
Values may be sent and summed in bfloat16 or wider, within the bound.
No kernel may reach another device: no remote copies, remote signals or barrier semaphores. Data moves between devices by JAX's collectives and lax.ppermute only.
A program may use at most 64 MiB of HBM per device.

```python
import math
import jax
import jax.numpy as jnp
from jax import lax

P_SIZE = 320
PAD = 640
S = 512
L = 4
NMOD = 8
NDIR = 4


def set_ends(values, key, low, top_value):
    extent = values.shape
    place = [jax.random.randint(jax.random.fold_in(key, axis), (), 0, extent[axis]) for axis in range(len(extent))]
    values = values.at[tuple(place)].set(low)
    longest = extent.index(max(extent))
    place[longest] = (place[longest] + 1) % extent[longest]
    return values.at[tuple(place)].set(top_value)


def steps_of(key, shape, pieces, least, largest):
    def one(dim, blocks):
        heights = jax.random.uniform(jax.random.fold_in(jax.random.fold_in(key, 6), dim), (blocks,), jnp.float32, least / len(pieces), largest / len(pieces))
        return jnp.repeat(jnp.exp(heights), shape[dim] // blocks).reshape((-1,) + (1,) * (len(shape) - dim - 1))

    gain = one(*pieces[0])
    for cut in pieces[1:]:
        gain = gain * one(*cut)
    return gain


def scatter_about(key, shape, spread, reach, split=(), kind=jnp.bfloat16):
    drawn = jax.random.normal(key, shape, jnp.float32) * spread
    if len(split) > 0:
        drawn = steps_of(key, shape, split, -0.22, 0.18) * drawn
    return jnp.clip(drawn, min=-reach, max=reach).astype(kind)


def setup_inputs(seed: int = 0, part: int = 0) -> dict:
    key_list = jax.random.split(jax.random.key(seed), 6)
    own_keys = jax.random.split(jax.random.fold_in(key_list[5], part), 6)
    return {
        "screens": scatter_about(own_keys[0], (L, S, S), 0.6, 6.0, ((1, 4),), jnp.float32),
        "footprint": set_ends(jax.random.randint(own_keys[1], (NDIR, L, 2), 0, S - P_SIZE), jax.random.fold_in(own_keys[1], 1), 0, (S - P_SIZE) - 1).astype(jnp.int32),
        "fraction": set_ends(jax.random.randint(own_keys[2], (NDIR, L, 2), 0, 16), jax.random.fold_in(own_keys[2], 1), 0, 15).astype(jnp.int32),
        "tilt_steps": set_ends(jax.random.randint(own_keys[3], (NMOD, 2), -64, 65), jax.random.fold_in(own_keys[3], 1), -64, 64).astype(jnp.int32),
        "facet_shift": set_ends(jax.random.randint(key_list[4], (4, 2), P_SIZE // 4, P_SIZE // 2 + 1), jax.random.fold_in(key_list[4], 1), P_SIZE // 4, (P_SIZE // 2 + 1) - 1).astype(jnp.int32),
    }


def as_wide(values):
    return lax.optimization_barrier(values).astype(jnp.float32)

def dft_table(count_out, count_in, direction_sign):
    out_ids = jnp.arange(count_out, dtype=jnp.int32) - count_out // 2
    in_ids = jnp.arange(count_in, dtype=jnp.int32) - count_in // 2
    turn_count = jnp.mod(out_ids[:, None] * in_ids[None, :], PAD)
    angle_map = direction_sign * 2.0 * math.pi / PAD * turn_count.astype(jnp.float32)
    normalizer = 1.0 / math.sqrt(PAD)
    return ((jnp.cos(angle_map) * normalizer).astype(jnp.bfloat16), (jnp.sin(angle_map) * normalizer).astype(jnp.bfloat16))

def left_stack(real_part, imag_part):
    return jnp.concatenate([jnp.concatenate([real_part, -imag_part], 1), jnp.concatenate([imag_part, real_part], 1)], 0)

def right_stack(real_part, imag_part):
    return jnp.concatenate([jnp.concatenate([real_part, imag_part], 1), jnp.concatenate([-imag_part, real_part], 1)], 0)

def pupil_amplitude(row_start, row_count):
    row_ids = row_start + jnp.arange(row_count, dtype=jnp.int32)
    col_ids = jnp.arange(P_SIZE, dtype=jnp.int32)
    along_y = 2 * row_ids - P_SIZE + 1
    along_x = 2 * col_ids - P_SIZE + 1
    radius_sq = along_y[:, None] * along_y[:, None] + along_x[None, :] * along_x[None, :]
    inner_edge = P_SIZE * 28 // 100 * (P_SIZE * 28 // 100)
    inside = (radius_sq <= P_SIZE * P_SIZE) & (radius_sq >= inner_edge)
    return inside.astype(jnp.float32)

def focal_mask(facet_shift):
    centred = jnp.arange(PAD, dtype=jnp.int32) - PAD // 2
    upper_half = (centred >= 0).astype(jnp.int32)
    quadrant = 2 * upper_half[:, None] + upper_half[None, :]
    shift_row = jnp.zeros((PAD, PAD), jnp.int32)
    shift_col = jnp.zeros((PAD, PAD), jnp.int32)
    for quad_idx in range(4):
        shift_row = shift_row + jnp.where(quadrant == quad_idx, facet_shift[quad_idx, 0], 0)
        shift_col = shift_col + jnp.where(quadrant == quad_idx, facet_shift[quad_idx, 1], 0)
    shift_row = shift_row * (2 * upper_half[:, None] - 1)
    shift_col = shift_col * (2 * upper_half[None, :] - 1)
    turn_count = jnp.mod(shift_row * centred[:, None] + shift_col * centred[None, :], PAD)
    angle_map = -2.0 * math.pi / PAD * turn_count.astype(jnp.float32)
    return (jnp.cos(angle_map), jnp.sin(angle_map))

def tilt_parts(tilt_table, row_ids, col_ids):
    turn_count = jnp.mod(tilt_table[:, 0, None, None] * row_ids[None, :, None] + tilt_table[:, 1, None, None] * col_ids[None, None, :], 8 * PAD)
    angle_map = 2.0 * math.pi / (8 * PAD) * turn_count.astype(jnp.float32)
    return (jnp.cos(angle_map), jnp.sin(angle_map))

def reference(screens, footprint, fraction, tilt_steps, facet_shift):
    d_re, d_im = dft_table(PAD, P_SIZE, -1.0)
    g_re, g_im = dft_table(PAD, PAD, 1.0)
    dl_big = as_wide(left_stack(d_re, d_im))
    dr_big = as_wide(right_stack(d_re.T, d_im.T))
    gl_big = as_wide(left_stack(g_re, g_im))
    gr_big = as_wide(right_stack(g_re, g_im))
    mask_cos, mask_sin = focal_mask(facet_shift)
    amplitude = pupil_amplitude(0, P_SIZE)
    row_ids = jnp.arange(P_SIZE, dtype=jnp.int32)

    def one_direction(inputs):
        offsets, fractions = inputs
        phase_map = jnp.zeros((P_SIZE, P_SIZE), jnp.float32)
        for layer_idx in range(L):
            window = lax.dynamic_slice(screens[layer_idx], (offsets[layer_idx, 0].astype(jnp.int32), offsets[layer_idx, 1].astype(jnp.int32)), (P_SIZE + 1, P_SIZE + 1))
            frac_row = fractions[layer_idx, 0].astype(jnp.float32) / 16.0
            frac_col = fractions[layer_idx, 1].astype(jnp.float32) / 16.0
            upper_rows = (1.0 - frac_col) * window[:-1, :-1] + frac_col * window[:-1, 1:]
            lower_rows = (1.0 - frac_col) * window[1:, :-1] + frac_col * window[1:, 1:]
            phase_map = phase_map + (1.0 - frac_row) * upper_rows + frac_row * lower_rows
        field_re = (amplitude * jnp.cos(phase_map)).astype(jnp.bfloat16)
        field_im = (amplitude * jnp.sin(phase_map)).astype(jnp.bfloat16)

        def one_point(running, tilt_row):
            tilt_cos, tilt_sin = tilt_parts(tilt_row[None, :], row_ids, row_ids)
            mod_re = (as_wide(field_re) * tilt_cos[0] - as_wide(field_im) * tilt_sin[0]).astype(jnp.bfloat16)
            mod_im = (as_wide(field_re) * tilt_sin[0] + as_wide(field_im) * tilt_cos[0]).astype(jnp.bfloat16)
            half_field = jnp.dot(dl_big, as_wide(jnp.concatenate([mod_re, mod_im], 0)), preferred_element_type=jnp.float32).astype(jnp.bfloat16)
            wide_half = jnp.concatenate([half_field[:PAD], half_field[PAD:]], 1)
            focal_field = jnp.dot(as_wide(wide_half), dr_big, preferred_element_type=jnp.float32)
            focal_re = focal_field[:, :PAD]
            focal_im = focal_field[:, PAD:]
            masked_re = (focal_re * mask_cos - focal_im * mask_sin).astype(jnp.bfloat16)
            masked_im = (focal_re * mask_sin + focal_im * mask_cos).astype(jnp.bfloat16)
            back_field = jnp.dot(gl_big, as_wide(jnp.concatenate([masked_re, masked_im], 0)), preferred_element_type=jnp.float32).astype(jnp.bfloat16)
            wide_back = jnp.concatenate([back_field[:PAD], back_field[PAD:]], 1)
            image_field = jnp.dot(as_wide(wide_back), gr_big, preferred_element_type=jnp.float32)
            image_re = image_field[:, :PAD]
            image_im = image_field[:, PAD:]
            return (running + image_re * image_re + image_im * image_im, None)
        running, _ = lax.scan(one_point, jnp.zeros((PAD, PAD), jnp.float32), tilt_steps)
        return running * (4.0 / NMOD)
    return lax.map(one_direction, (footprint, fraction))
```

```python
import functools

import jax
import jax.numpy as jnp
from jax import lax
from jax.experimental import pallas as pl
from jax.experimental.pallas import tpu as pltpu
from jax.sharding import PartitionSpec as P

P_SIZE = 320
PAD = 640
HALF = P_SIZE // 2
FINE = 8 * PAD
CENTRE = 2 * (PAD - 2)
F32 = jnp.float32
BF16 = jnp.bfloat16
I32 = jnp.int32
I16 = jnp.int16
SIN_TERMS = (6.283184916, -41.34158923, 81.59994333, -76.61447253, 41.34288235, -12.47124354)
COS_TERMS = (0.9999992108, -19.73898036, 64.92865742, -85.27162153, 58.79049212, -21.07110563)


def round_up(value, step):
    return (value + step - 1) // step * step


def horner(terms, square):
    total = jnp.full_like(square, terms[-1])
    for term in terms[-2::-1]:
        total = total * square + term
    return total


def cos_sin(turns):
    square = turns * turns
    return horner(COS_TERMS, square), horner(SIN_TERMS, square) * turns


def centred(turns):
    return turns - jnp.floor(turns + 0.5)


def iota(shape, axis):
    return lax.broadcasted_iota(I32, shape, axis)


def lane_vector(values, index):
    out = jnp.zeros(index.shape, values[0].dtype)
    for place, value in enumerate(values):
        out = jnp.where(index == place, value, out)
    return out


def phase_kernel(foot, frac, tilt, screens, keep, send, *, lanes):
    layers, band, width = screens.shape
    points = tilt.shape[0]
    me = lax.axis_index("mod")
    high, low = [], []
    for layer in range(layers):
        start = foot[0, layer, 1]
        part = frac[0, layer, 1].astype(F32) * (1.0 / 16.0)
        rows = screens[layer]
        here = pltpu.roll(rows, lax.rem(width - start, width), 1)[:, :lanes]
        after = pltpu.roll(rows, width - 1 - start, 1)[:, :lanes]
        mixed = here * (1.0 - part) + after * part
        top = mixed.astype(BF16)
        high.append(top)
        low.append((mixed - top.astype(F32)).astype(BF16))
    index = iota((1, layers * band), 1)
    layer_of = index // band
    first = lane_vector([foot[0, i, 0] for i in range(layers)], layer_of)
    part = lane_vector([frac[0, i, 0].astype(F32) * (1.0 / 16.0) for i in range(layers)], layer_of)
    offset = me * band + index - layer_of * band - first
    delta = offset - iota((P_SIZE, layers * band), 0)
    pick = jnp.where(delta == 0, 1.0 - part, jnp.where(delta == 1, part, 0.0)).astype(BF16)
    total = jnp.dot(pick, jnp.concatenate(high, 0), preferred_element_type=F32)
    total = total + jnp.dot(pick, jnp.concatenate(low, 0), preferred_element_type=F32)
    coded = jnp.floor(total * (65536.0 / 6.283185307179586) + 0.5).astype(I32)
    coded = lax.shift_right_arithmetic(lax.shift_left(coded, 16), 16)
    row = iota((HALF, lanes), 0)
    lane = iota((HALF, lanes), 1)
    table = jnp.zeros((HALF, lanes), I32)
    for point in range(points):
        place = me * points + point
        table = jnp.where((lane == P_SIZE + place) & (row == HALF - 1), tilt[point, 0], table)
        table = jnp.where((lane == lanes - 1) & (row == place), tilt[point, 1], table)
    upper = jnp.where(lane < P_SIZE, coded[:HALF], table)
    lower = jnp.where(lane < P_SIZE, coded[HALF:], table)
    odd = lax.rem(me, 2) == 1
    keep[...] = jnp.where(odd, lower, upper).astype(I16)
    send[...] = jnp.where(odd, upper, lower).astype(I16)


def dirichlet(steps, flip):
    size = jnp.abs(steps)
    near = jnp.minimum(size, PAD - size)
    turns = near.astype(F32) * (0.5 / PAD)
    sine = horner(SIN_TERMS, turns * turns) * turns
    quarter = jnp.bitwise_and(steps, 3)
    negative = (quarter == 3) != ((steps < 0) != flip)
    value = 1.0 / (jnp.where(negative, -float(PAD), float(PAD)) * sine)
    odd = jnp.bitwise_and(steps, 1) == 1
    return jnp.where(odd, value, jnp.where(steps == 0, 0.5, 0.0)).astype(BF16)


def shift_of(facet, quadrant, axis):
    side = quadrant // 2 if axis == 0 else quadrant % 2
    return facet[quadrant, axis] * (2 * side - 1), side == 0


def table_kernel(facet, left, right, *, rows, padded, lanes):
    first = lax.axis_index("mod") * rows
    for quadrant in range(4):
        shift, flip = shift_of(facet, quadrant, 0)
        steps = iota((padded, P_SIZE), 0) - iota((padded, P_SIZE), 1) + (first - HALF - shift)
        left[pl.ds(quadrant * padded, padded), :] = dirichlet(steps, flip)
        shift, flip = shift_of(facet, quadrant, 1)
        source = iota((lanes, PAD), 0)
        steps = iota((lanes, PAD), 1) - source + (-HALF - shift)
        value = dirichlet(steps, flip)
        right[pl.ds(quadrant * lanes, lanes), :] = jnp.where(source < P_SIZE, value, 0.0).astype(BF16)


def image_kernel(
    facet, own, other, left, right, out, row_re, row_im, col_re, col_im, field_re, field_im, total, *, count, padded, lanes
):
    me = lax.axis_index("mod")
    odd = lax.rem(me, 2) == 1
    mine = own[...].astype(I32)
    theirs = other[...].astype(I32)
    coded = jnp.concatenate([jnp.where(odd, theirs, mine), jnp.where(odd, mine, theirs)], 0)
    wave_re, wave_im = cos_sin(coded.astype(F32) * (1.0 / 65536.0))
    along_y = 2 * iota((P_SIZE, lanes), 0) - (P_SIZE - 1)
    along_x = 2 * iota((P_SIZE, lanes), 1) - (P_SIZE - 1)
    radius = along_y * along_y + along_x * along_x
    edge = P_SIZE * 28 // 100
    inside = (radius <= P_SIZE * P_SIZE) & (radius >= edge * edge)
    field_re[...] = jnp.where(inside, wave_re, 0.0)
    field_im[...] = jnp.where(inside, wave_im, 0.0)
    base = P_SIZE // 128 * 128
    tilt_row = mine[HALF - 1 : HALF, base : base + 128]
    steps = (tilt_row - CENTRE) * iota((P_SIZE, 128), 0)
    cos_rows, sin_rows = cos_sin(centred(steps.astype(F32) * (1.0 / FINE)))
    for point in range(count):
        place = P_SIZE - base + point
        row_re[point] = jnp.broadcast_to(cos_rows[:, place : place + 1], (P_SIZE, 128))
        row_im[point] = jnp.broadcast_to(sin_rows[:, place : place + 1], (P_SIZE, 128))
    quad = iota((8, 1), 0)
    facet_steps = jnp.zeros((8, 1), I32)
    for quadrant in range(4):
        shift = shift_of(facet, quadrant, 0)[0] + shift_of(facet, quadrant, 1)[0]
        facet_steps = jnp.where(quad == quadrant, shift * (-2 * (PAD - 2)), facet_steps)
    for point in range(count):
        tilt_col = mine[point : point + 1, lanes - 1 : lanes]
        steps = (tilt_col - CENTRE) * iota((8, lanes), 1) + facet_steps
        turn_re, turn_im = cos_sin(centred(steps.astype(F32) * (1.0 / FINE)))
        col_re[point] = turn_re
        col_im[point] = turn_im
    total[...] = jnp.zeros_like(total)

    def one_point(point, carry):
        copies = lanes // 128
        turn_re = jnp.concatenate([row_re[point]] * copies, 1)
        turn_im = jnp.concatenate([row_im[point]] * copies, 1)
        wide_re, wide_im = field_re[...], field_im[...]
        moved_re = (wide_re * turn_re - wide_im * turn_im).astype(BF16)
        moved_im = (wide_re * turn_im + wide_im * turn_re).astype(BF16)
        half = jnp.dot(left[...], jnp.concatenate([moved_re, moved_im], 1), preferred_element_type=F32)
        parts_re, parts_im = [], []
        for quadrant in range(4):
            piece = half[quadrant * padded : (quadrant + 1) * padded]
            piece_re, piece_im = piece[:, :lanes], piece[:, lanes:]
            turn_re = col_re[point, quadrant : quadrant + 1, :]
            turn_im = col_im[point, quadrant : quadrant + 1, :]
            parts_re.append((piece_re * turn_re - piece_im * turn_im).astype(BF16))
            parts_im.append((piece_re * turn_im + piece_im * turn_re).astype(BF16))
        stacked = jnp.concatenate([jnp.concatenate(parts_re, 1), jnp.concatenate(parts_im, 1)], 0)
        image = jnp.dot(stacked, right[...], preferred_element_type=F32)
        image_re, image_im = image[:padded], image[padded:]
        total[...] += image_re * image_re + image_im * image_im
        return carry

    lax.fori_loop(0, count, one_point, 0)
    out[0] = total[: out.shape[1]] * (4.0 / count)


def swapped(values, peers, step):
    return lax.ppermute(values, "mod", [(i, i ^ step) for i in range(peers)])


def shards(screens, footprint, fraction, tilt_steps, facet_shift):
    peers = lax.axis_size("mod")
    layers, band, width = screens.shape
    count = tilt_steps.shape[0] * peers
    rows = PAD // peers
    padded = round_up(rows, 16)
    lanes = round_up(P_SIZE + count + 1, 128)
    smem = pl.BlockSpec(memory_space=pltpu.SMEM)
    vmem = pl.BlockSpec(memory_space=pltpu.VMEM)
    params = pltpu.CompilerParams(vmem_limit_bytes=40 * 1024 * 1024)
    half_shape = jax.ShapeDtypeStruct((HALF, lanes), I16)
    keep, send = pl.pallas_call(
        functools.partial(phase_kernel, lanes=lanes),
        out_shape=(half_shape, half_shape),
        in_specs=[smem, smem, smem, vmem],
        out_specs=(vmem, vmem),
        compiler_params=params,
        name="phase_parts",
    )(footprint, fraction, tilt_steps, screens)
    left, right = pl.pallas_call(
        functools.partial(table_kernel, rows=rows, padded=padded, lanes=lanes),
        out_shape=(
            jax.ShapeDtypeStruct((4 * padded, P_SIZE), BF16),
            jax.ShapeDtypeStruct((4 * lanes, PAD), BF16),
        ),
        in_specs=[smem],
        out_specs=(vmem, vmem),
        compiler_params=params,
        cost_estimate=pl.CostEstimate(flops=30_000_000, bytes_accessed=2_500_000, transcendentals=0),
        name="half_band_tables",
    )(facet_shift)
    own = keep + swapped(send, peers, 1)
    step = 2
    while step < peers:
        own = own + swapped(own, peers, step)
        step *= 2
    other = swapped(own, peers, 1)
    return pl.pallas_call(
        functools.partial(image_kernel, count=count, padded=padded, lanes=lanes),
        out_shape=jax.ShapeDtypeStruct((1, rows, PAD), F32),
        in_specs=[smem, vmem, vmem, vmem, vmem],
        out_specs=vmem,
        scratch_shapes=[
            pltpu.VMEM((count, P_SIZE, 128), F32),
            pltpu.VMEM((count, P_SIZE, 128), F32),
            pltpu.VMEM((count, 8, lanes), F32),
            pltpu.VMEM((count, 8, lanes), F32),
            pltpu.VMEM((P_SIZE, lanes), F32),
            pltpu.VMEM((P_SIZE, lanes), F32),
            pltpu.VMEM((padded, PAD), F32),
        ],
        compiler_params=params,
        name="detector_rows",
    )(facet_shift, own, other, left, right)


def solution(mesh):
    placed = (
        P("group", "mod", None),
        P(("group", "dir"), None, None),
        P(("group", "dir"), None, None),
        P(("group", "mod"), None),
        P(),
    )
    return jax.shard_map(
        shards,
        mesh=mesh,
        in_specs=placed,
        out_specs=P(("group", "dir"), "mod", None),
        check_vma=False,
    )
```

```python
import functools

import jax
import jax.numpy as jnp
import numpy as np
from jax import lax
from jax.experimental import pallas as pl
from jax.experimental.pallas import tpu as pltpu
from jax.sharding import PartitionSpec as P

P_SIZE = 320
PAD = 640
HALF = P_SIZE // 2
FINE = 8 * PAD
CENTRE = 2 * (PAD - 2)
F32 = jnp.float32
BF16 = jnp.bfloat16
I32 = jnp.int32
I16 = jnp.int16
SIN_TERMS = (6.283184916, -41.34158923, 81.59994333, -76.61447253, 41.34288235, -12.47124354)
COS_TERMS = (0.9999992108, -19.73898036, 64.92865742, -85.27162153, 58.79049212, -21.07110563)


def round_up(value, step):
    return (value + step - 1) // step * step


def horner(terms, square):
    total = jnp.full_like(square, terms[-1])
    for term in terms[-2::-1]:
        total = total * square + term
    return total


def cos_sin(turns):
    square = turns * turns
    return horner(COS_TERMS, square), horner(SIN_TERMS, square) * turns


def centred(turns):
    return turns - jnp.floor(turns + 0.5)


def iota(shape, axis):
    return lax.broadcasted_iota(I32, shape, axis)


def lane_vector(values, index):
    out = jnp.zeros(index.shape, values[0].dtype)
    for place, value in enumerate(values):
        out = jnp.where(index == place, value, out)
    return out


def phase_kernel(
    foot_hbm, frac_hbm, tilt_hbm, screens_hbm, keep, send, foot, frac, tilt, screens, small_sems, layer_sems, *, lanes
):
    layers, band, width = screens.shape
    points = tilt.shape[0]
    me = lax.axis_index("mod")
    small = [
        pltpu.make_async_copy(source, target, small_sems.at[place])
        for place, (source, target) in enumerate(((foot_hbm, foot), (frac_hbm, frac), (tilt_hbm, tilt)))
    ]
    large = [
        pltpu.make_async_copy(screens_hbm.at[layer], screens.at[layer], layer_sems.at[layer])
        for layer in range(layers)
    ]
    for copy in small + large:
        copy.start()
    for copy in small:
        copy.wait()
    index = iota((1, layers * band), 1)
    layer_of = index // band
    first = lane_vector([foot[0, 0, i] for i in range(layers)], layer_of)
    part = lane_vector([frac[0, 0, i].astype(F32) * (1.0 / 16.0) for i in range(layers)], layer_of)
    offset = me * band + index - layer_of * band - first
    delta = offset - iota((P_SIZE, layers * band), 0)
    pick = jnp.where(delta == 0, 1.0 - part, jnp.where(delta == 1, part, 0.0)).astype(BF16)
    high, low = [], []
    for layer in range(layers):
        start = foot[0, 1, layer]
        part = frac[0, 1, layer].astype(F32) * (1.0 / 16.0)
        large[layer].wait()
        rows = screens[layer]
        here = pltpu.roll(rows, lax.rem(width - start, width), 1)[:, :lanes]
        after = pltpu.roll(rows, width - 1 - start, 1)[:, :lanes]
        mixed = here * (1.0 - part) + after * part
        top = mixed.astype(BF16)
        high.append(top)
        low.append((mixed - top.astype(F32)).astype(BF16))
    total = jnp.dot(pick, jnp.concatenate(high, 0), preferred_element_type=F32)
    total = total + jnp.dot(pick, jnp.concatenate(low, 0), preferred_element_type=F32)
    coded = jnp.floor(total * (65536.0 / 6.283185307179586) + 0.5).astype(I32)
    coded = lax.shift_right_arithmetic(lax.shift_left(coded, 16), 16)
    row = iota((HALF, lanes), 0)
    lane = iota((HALF, lanes), 1)
    table = jnp.zeros((HALF, lanes), I32)
    for point in range(points):
        place = me * points + point
        table = jnp.where((lane == P_SIZE + place) & (row == HALF - 1), tilt[point, 0], table)
        table = jnp.where((lane == lanes - 1) & (row == place), tilt[point, 1], table)
    upper = jnp.where(lane < P_SIZE, coded[:HALF], table)
    lower = jnp.where(lane < P_SIZE, coded[HALF:], table)
    odd = lax.rem(me, 2) == 1
    keep[...] = jnp.where(odd, lower, upper).astype(I16)
    send[...] = jnp.where(odd, upper, lower).astype(I16)


def shift_of(facet, quadrant, axis):
    side = quadrant // 2 if axis == 0 else quadrant % 2
    return facet[axis, quadrant] * (2 * side - 1), side == 0


def half_band():
    steps = np.arange(PAD + P_SIZE + 24)[:, None] - P_SIZE - np.arange(PAD)[None, :]
    odd = (steps % 2 != 0) & (np.abs(steps) < PAD)
    sine = np.sin(np.pi / PAD * np.where(odd, steps, 1))
    value = np.where(odd, (2 - steps % 4) / (PAD * sine), np.where(steps == 0, 0.5, 0.0))
    return value.astype(jnp.bfloat16).astype(np.float32)


def window(band, start, count, width):
    whole = lax.shift_right_logical(start, 3) * 8
    block = band[pl.ds(pl.multiple_of(whole, 8), count + 8), :width]
    return pltpu.roll(block, count + 8 - (start - whole), 0)[:count]


def table_kernel(facet_hbm, band, own, left, right, turns, passed, facet, sem, *, rows, padded, lanes):
    copy = pltpu.make_async_copy(facet_hbm, facet, sem)
    copy.start()
    passed[...] = own[...]
    copy.wait()
    first = lax.axis_index("mod") * rows
    signs = 1.0 - 2.0 * jnp.bitwise_and(iota((8, PAD), 0) + iota((8, PAD), 1), 1).astype(F32)
    quad = iota((8, lanes), 0)
    facet_steps = jnp.zeros((8, lanes), I32)
    for quadrant in range(4):
        row_shift, row_flip = shift_of(facet, quadrant, 0)
        col_shift, col_flip = shift_of(facet, quadrant, 1)
        start = first + HALF - row_shift
        piece = window(band, start, padded, P_SIZE)
        if row_flip:
            flips = signs[:, :P_SIZE] * (1 - 2 * jnp.bitwise_and(start, 1)).astype(F32)
            piece = piece * jnp.concatenate([flips] * (padded // 8), 0)
        left[pl.ds(quadrant * padded, padded), :] = piece.astype(BF16)
        start = col_shift + (HALF + P_SIZE)
        piece = window(band, start, P_SIZE, PAD)
        if col_flip:
            flips = signs * (1 - 2 * jnp.bitwise_and(start, 1)).astype(F32)
            piece = piece * jnp.concatenate([flips] * (P_SIZE // 8), 0)
        right[pl.ds(quadrant * lanes, P_SIZE), :] = piece.astype(BF16)
        right[pl.ds(quadrant * lanes + P_SIZE, lanes - P_SIZE), :] = jnp.zeros((lanes - P_SIZE, PAD), BF16)
        facet_steps = jnp.where(quad == quadrant, (row_shift + col_shift) * (-2 * (PAD - 2)), facet_steps)
    turns[...] = facet_steps


def image_kernel(
    facet_steps, own, other, left, right, out, row_re, row_im, col_re, col_im, field_re, field_im, total, *, count, padded, lanes
):
    me = lax.axis_index("mod")
    odd = lax.rem(me, 2) == 1
    mine = own[...].astype(I32)
    theirs = other[...].astype(I32)
    coded = jnp.concatenate([jnp.where(odd, theirs, mine), jnp.where(odd, mine, theirs)], 0)
    wave_re, wave_im = cos_sin(coded.astype(F32) * (1.0 / 65536.0))
    along_y = 2 * iota((P_SIZE, lanes), 0) - (P_SIZE - 1)
    along_x = 2 * iota((P_SIZE, lanes), 1) - (P_SIZE - 1)
    radius = along_y * along_y + along_x * along_x
    edge = P_SIZE * 28 // 100
    inside = (radius <= P_SIZE * P_SIZE) & (radius >= edge * edge)
    field_re[...] = jnp.where(inside, wave_re, 0.0)
    field_im[...] = jnp.where(inside, wave_im, 0.0)
    base = P_SIZE // 128 * 128
    tilt_row = mine[HALF - 1 : HALF, base : base + 128]
    steps = (tilt_row - CENTRE) * iota((P_SIZE, 128), 0)
    cos_rows, sin_rows = cos_sin(centred(steps.astype(F32) * (1.0 / FINE)))
    for point in range(count):
        place = P_SIZE - base + point
        row_re[point] = jnp.broadcast_to(cos_rows[:, place : place + 1], (P_SIZE, 128))
        row_im[point] = jnp.broadcast_to(sin_rows[:, place : place + 1], (P_SIZE, 128))
    for point in range(count):
        tilt_col = mine[point : point + 1, lanes - 1 : lanes]
        steps = (tilt_col - CENTRE) * iota((8, lanes), 1) + facet_steps[...]
        turn_re, turn_im = cos_sin(centred(steps.astype(F32) * (1.0 / FINE)))
        col_re[point] = turn_re
        col_im[point] = turn_im
    total[...] = jnp.zeros_like(total)

    def one_point(point, carry):
        copies = lanes // 128
        turn_re = jnp.concatenate([row_re[point]] * copies, 1)
        turn_im = jnp.concatenate([row_im[point]] * copies, 1)
        wide_re, wide_im = field_re[...], field_im[...]
        moved_re = (wide_re * turn_re - wide_im * turn_im).astype(BF16)
        moved_im = (wide_re * turn_im + wide_im * turn_re).astype(BF16)
        half = jnp.dot(left[...], jnp.concatenate([moved_re, moved_im], 1), preferred_element_type=F32)
        parts_re, parts_im = [], []
        for quadrant in range(4):
            piece = half[quadrant * padded : (quadrant + 1) * padded]
            piece_re, piece_im = piece[:, :lanes], piece[:, lanes:]
            turn_re = col_re[point, quadrant : quadrant + 1, :]
            turn_im = col_im[point, quadrant : quadrant + 1, :]
            parts_re.append((piece_re * turn_re - piece_im * turn_im).astype(BF16))
            parts_im.append((piece_re * turn_im + piece_im * turn_re).astype(BF16))
        stacked = jnp.concatenate([jnp.concatenate(parts_re, 1), jnp.concatenate(parts_im, 1)], 0)
        image = jnp.dot(stacked, right[...], preferred_element_type=F32)
        image_re, image_im = image[:padded], image[padded:]
        total[...] += image_re * image_re + image_im * image_im
        return carry

    lax.fori_loop(0, count, one_point, 0, unroll=min(count, 8))
    out[0] = total[: out.shape[1]] * (4.0 / count)


def swapped(values, peers, step):
    return lax.ppermute(values, "mod", [(i, i ^ step) for i in range(peers)])


def shards(screens, footprint, fraction, tilt_steps, facet_shift):
    peers = lax.axis_size("mod")
    layers, band, width = screens.shape
    count = tilt_steps.shape[0] * peers
    rows = PAD // peers
    padded = round_up(rows, 16)
    lanes = round_up(P_SIZE + count + 1, 128)
    hbm = pl.BlockSpec(memory_space=pltpu.HBM)
    vmem = pl.BlockSpec(memory_space=pltpu.VMEM)
    params = pltpu.CompilerParams(vmem_limit_bytes=40 * 1024 * 1024)
    half_shape = jax.ShapeDtypeStruct((HALF, lanes), I16)
    keep, send = pl.pallas_call(
        functools.partial(phase_kernel, lanes=lanes),
        out_shape=(half_shape, half_shape),
        in_specs=[hbm, hbm, hbm, hbm],
        out_specs=(vmem, vmem),
        scratch_shapes=[
            pltpu.SMEM((1, 2, layers), I32),
            pltpu.SMEM((1, 2, layers), I32),
            pltpu.SMEM(tilt_steps.shape, I32),
            pltpu.VMEM(screens.shape, F32),
            pltpu.SemaphoreType.DMA((3,)),
            pltpu.SemaphoreType.DMA((layers,)),
        ],
        compiler_params=pltpu.CompilerParams(vmem_limit_bytes=60 * 1024 * 1024),
        name="phase_parts",
    )(footprint.swapaxes(1, 2), fraction.swapaxes(1, 2), tilt_steps, screens)
    own = keep + swapped(send, peers, 1)
    left, right, turns, passed = pl.pallas_call(
        functools.partial(table_kernel, rows=rows, padded=padded, lanes=lanes),
        out_shape=(
            jax.ShapeDtypeStruct((4 * padded, P_SIZE), BF16),
            jax.ShapeDtypeStruct((4 * lanes, PAD), BF16),
            jax.ShapeDtypeStruct((8, lanes), I32),
            half_shape,
        ),
        in_specs=[hbm, vmem, vmem],
        out_specs=(vmem, vmem, vmem, vmem),
        scratch_shapes=[pltpu.SMEM((2, 4), I32), pltpu.SemaphoreType.DMA(())],
        compiler_params=params,
        cost_estimate=pl.CostEstimate(flops=5_000_000_000, bytes_accessed=20_000_000, transcendentals=0),
        name="half_band_tables",
    )(facet_shift.T, jnp.asarray(half_band()), own)
    step = 2
    while step < peers:
        own = passed = passed + swapped(own, peers, step)
        step *= 2
    other = swapped(own, peers, 1)
    return pl.pallas_call(
        functools.partial(image_kernel, count=count, padded=padded, lanes=lanes),
        out_shape=jax.ShapeDtypeStruct((1, rows, PAD), F32),
        in_specs=[vmem, vmem, vmem, vmem, vmem],
        out_specs=vmem,
        scratch_shapes=[
            pltpu.VMEM((count, P_SIZE, 128), F32),
            pltpu.VMEM((count, P_SIZE, 128), F32),
            pltpu.VMEM((count, 8, lanes), F32),
            pltpu.VMEM((count, 8, lanes), F32),
            pltpu.VMEM((P_SIZE, lanes), F32),
            pltpu.VMEM((P_SIZE, lanes), F32),
            pltpu.VMEM((padded, PAD), F32),
        ],
        compiler_params=params,
        name="detector_rows",
    )(turns, own, other, left, right)


def solution(mesh):
    placed = (
        P("group", "mod", None),
        P(("group", "dir"), None, None),
        P(("group", "dir"), None, None),
        P(("group", "mod"), None),
        P(),
    )
    return jax.shard_map(
        shards,
        mesh=mesh,
        in_specs=placed,
        out_specs=P(("group", "dir"), "mod", None),
        check_vma=False,
    )
```

```python
import functools
import math

import jax
import jax.numpy as jnp
from jax import lax
from jax.experimental import pallas as pl
from jax.experimental.pallas import tpu as pltpu
from jax.sharding import PartitionSpec as P

P_SIZE = 320
PAD = 640
HALF = P_SIZE // 2
FINE = 8 * PAD
CENTRE = 2 * (PAD - 2)
F32 = jnp.float32
BF16 = jnp.bfloat16
I32 = jnp.int32
I16 = jnp.int16
SIN_TERMS = (6.283184916, -41.34158923, 81.59994333, -76.61447253, 41.34288235, -12.47124354)
COS_TERMS = (0.9999992108, -19.73898036, 64.92865742, -85.27162153, 58.79049212, -21.07110563)


def round_up(value, step):
    return (value + step - 1) // step * step


def horner(terms, square):
    total = jnp.full_like(square, terms[-1])
    for term in terms[-2::-1]:
        total = total * square + term
    return total


def cos_sin(turns):
    square = turns * turns
    return horner(COS_TERMS, square), horner(SIN_TERMS, square) * turns


def centred(turns):
    return turns - jnp.floor(turns + 0.5)


def iota(shape, axis):
    return lax.broadcasted_iota(I32, shape, axis)


def lane_vector(values, index):
    out = jnp.zeros(index.shape, values[0].dtype)
    for place, value in enumerate(values):
        out = jnp.where(index == place, value, out)
    return out


def phase_kernel(
    foot_hbm, frac_hbm, tilt_hbm, screens_hbm, keep, send, foot, frac, tilt, screens, small_sems, layer_sems, *, lanes
):
    layers, band, width = screens.shape
    points = tilt.shape[0]
    me = lax.axis_index("mod")
    small = [
        pltpu.make_async_copy(source, target, small_sems.at[place])
        for place, (source, target) in enumerate(((foot_hbm, foot), (frac_hbm, frac), (tilt_hbm, tilt)))
    ]
    large = [
        pltpu.make_async_copy(screens_hbm.at[layer], screens.at[layer], layer_sems.at[layer])
        for layer in range(layers)
    ]
    for copy in small + large:
        copy.start()
    for copy in small:
        copy.wait()
    index = iota((1, layers * band), 1)
    layer_of = index // band
    first = lane_vector([foot[0, 0, i] for i in range(layers)], layer_of)
    part = lane_vector([frac[0, 0, i].astype(F32) * (1.0 / 16.0) for i in range(layers)], layer_of)
    offset = me * band + index - layer_of * band - first
    delta = offset - iota((P_SIZE, layers * band), 0)
    pick = jnp.where(delta == 0, 1.0 - part, jnp.where(delta == 1, part, 0.0)).astype(BF16)
    high, low = [], []
    for layer in range(layers):
        start = foot[0, 1, layer]
        part = frac[0, 1, layer].astype(F32) * (1.0 / 16.0)
        large[layer].wait()
        rows = screens[layer]
        here = pltpu.roll(rows, lax.rem(width - start, width), 1)[:, :lanes]
        after = pltpu.roll(rows, width - 1 - start, 1)[:, :lanes]
        mixed = here * (1.0 - part) + after * part
        top = mixed.astype(BF16)
        high.append(top)
        low.append((mixed - top.astype(F32)).astype(BF16))
    total = jnp.dot(pick, jnp.concatenate(high, 0), preferred_element_type=F32)
    total = total + jnp.dot(pick, jnp.concatenate(low, 0), preferred_element_type=F32)
    coded = jnp.floor(total * (65536.0 / 6.283185307179586) + 0.5).astype(I32)
    coded = lax.shift_right_arithmetic(lax.shift_left(coded, 16), 16)
    row = iota((HALF, lanes), 0)
    lane = iota((HALF, lanes), 1)
    table = jnp.zeros((HALF, lanes), I32)
    for point in range(points):
        place = me * points + point
        table = jnp.where((lane == P_SIZE + place) & (row == HALF - 1), tilt[point, 0], table)
        table = jnp.where((lane == lanes - 1) & (row == place), tilt[point, 1], table)
    upper = jnp.where(lane < P_SIZE, coded[:HALF], table)
    lower = jnp.where(lane < P_SIZE, coded[HALF:], table)
    odd = lax.rem(me, 2) == 1
    keep[...] = jnp.where(odd, lower, upper).astype(I16)
    send[...] = jnp.where(odd, upper, lower).astype(I16)


def shift_of(facet, quadrant, axis):
    side = quadrant // 2 if axis == 0 else quadrant % 2
    return facet[axis, quadrant] * (2 * side - 1), side == 0


def dirichlet(steps, flip):
    size = jnp.abs(steps)
    near = jnp.minimum(size, PAD - size)
    turns = near.astype(F32) * (0.5 / PAD)
    sine = horner(SIN_TERMS, turns * turns) * turns
    negative = ((jnp.bitwise_and(steps, 3) == 3) != (steps < 0)) != flip
    value = 1.0 / (jnp.where(negative, -float(PAD), float(PAD)) * sine)
    odd = jnp.bitwise_and(steps, 1) == 1
    return jnp.where(odd, value, jnp.where(steps == 0, 0.5, 0.0))


def toeplitz(top, flip, rows, width):
    lane = iota((8, width), 1)
    lane = jnp.where(lane >= width - rows, lane - width, lane)
    first = dirichlet(top - lane, flip)
    return pltpu.roll(jnp.concatenate([first] * (rows // 8), 0), 0, 1, stride=1, stride_axis=0)


def table_kernel(facet_hbm, own, left, right, turns, passed, facet, sem, *, rows, padded, lanes):
    copy = pltpu.make_async_copy(facet_hbm, facet, sem)
    copy.start()
    passed[...] = own[...]
    copy.wait()
    first = lax.axis_index("mod") * rows
    quad = iota((8, lanes), 0)
    facet_steps = jnp.zeros((8, lanes), I32)
    blocks = PAD // 128
    spill = P_SIZE % 128
    whole = P_SIZE // 128
    narrow = round_up(P_SIZE + padded, 128)
    wide = (2 * blocks - 1) * 128
    for quadrant in range(4):
        row_shift, row_flip = shift_of(facet, quadrant, 0)
        col_shift, col_flip = shift_of(facet, quadrant, 1)
        piece = toeplitz(first - HALF - row_shift, row_flip, padded, narrow)
        left[pl.ds(quadrant * padded, padded), :] = piece[:, :P_SIZE].astype(BF16)
        facet_steps = jnp.where(quad == quadrant, (row_shift + col_shift) * (-2 * (PAD - 2)), facet_steps)
    turns[...] = facet_steps
    lane = iota((128, 128), 1)
    for pair in range(2):
        pieces = []
        for side in range(2):
            col_shift, col_flip = shift_of(facet, 2 * pair + side, 1)
            top = (blocks - 1) * 128 + side * spill - HALF - col_shift
            pieces.append(toeplitz(top, col_flip, 128, wide))
        for block in range(blocks):
            even, odd = (piece[:, (blocks - 1 - block) * 128 :] for piece in pieces)
            edge = jnp.where(lane < spill, even[:, whole * 128 : whole * 128 + 128], odd[:, :128])
            joined = [even[:, : whole * 128], edge, odd[:, 128 : whole * 128 + 128]]
            right[pl.ds(block * 128, 128), pl.ds(pair * 2 * P_SIZE, 2 * P_SIZE)] = jnp.concatenate(joined, 1).astype(BF16)


def image_kernel(
    facet_steps, own, other, left, right, out, row_re, row_im, col_re, col_im, field_re, field_im, total, *, count, group, padded, lanes
):
    me = lax.axis_index("mod")
    odd = lax.rem(me, 2) == 1
    mine = own[...].astype(I32)
    theirs = other[...].astype(I32)
    coded = jnp.concatenate([jnp.where(odd, theirs, mine), jnp.where(odd, mine, theirs)], 0)
    wave_re, wave_im = cos_sin(coded.astype(F32) * (1.0 / 65536.0))
    along_y = 2 * iota((P_SIZE, lanes), 0) - (P_SIZE - 1)
    along_x = 2 * iota((P_SIZE, lanes), 1) - (P_SIZE - 1)
    radius = along_y * along_y + along_x * along_x
    edge = P_SIZE * 28 // 100
    inside = (radius <= P_SIZE * P_SIZE) & (radius >= edge * edge)
    field_re[...] = jnp.where(inside, wave_re, 0.0)
    field_im[...] = jnp.where(inside, wave_im, 0.0)
    base = P_SIZE // 128 * 128
    tilt_row = mine[HALF - 1 : HALF, base : base + 128]
    steps = (tilt_row - CENTRE) * iota((P_SIZE, 128), 0)
    cos_rows, sin_rows = cos_sin(centred(steps.astype(F32) * (1.0 / FINE)))
    for point in range(count):
        place = P_SIZE - base + point
        row_re[point] = jnp.broadcast_to(cos_rows[:, place : place + 1], (P_SIZE, 128))
        row_im[point] = jnp.broadcast_to(sin_rows[:, place : place + 1], (P_SIZE, 128))
    for point in range(count):
        tilt_col = mine[point : point + 1, lanes - 1 : lanes]
        steps = (tilt_col - CENTRE) * iota((8, lanes), 1) + facet_steps[...]
        turn_re, turn_im = cos_sin(centred(steps.astype(F32) * (1.0 / FINE)))
        col_re[point] = turn_re
        col_im[point] = turn_im
    total[...] = jnp.zeros_like(total)

    def one_group(index, carry):
        copies = lanes // 128
        stacked = []
        for member in range(group):
            point = index * group + member
            turn_re = jnp.concatenate([row_re[point]] * copies, 1)
            turn_im = jnp.concatenate([row_im[point]] * copies, 1)
            wide_re, wide_im = field_re[...], field_im[...]
            moved_re = (wide_re * turn_re - wide_im * turn_im).astype(BF16)
            moved_im = (wide_re * turn_im + wide_im * turn_re).astype(BF16)
            half = jnp.dot(left[...], jnp.concatenate([moved_re, moved_im], 1), preferred_element_type=F32)
            parts_re, parts_im = [], []
            for quadrant in range(4):
                piece = half[quadrant * padded : (quadrant + 1) * padded]
                piece_re, piece_im = piece[:, :lanes], piece[:, lanes:]
                turn_re = col_re[point, quadrant : quadrant + 1, :]
                turn_im = col_im[point, quadrant : quadrant + 1, :]
                parts_re.append((piece_re * turn_re - piece_im * turn_im).astype(BF16)[:, :P_SIZE])
                parts_im.append((piece_re * turn_im + piece_im * turn_re).astype(BF16)[:, :P_SIZE])
            stacked += [jnp.concatenate(parts_re, 1), jnp.concatenate(parts_im, 1)]
        image = lax.dot_general(
            right[...], jnp.concatenate(stacked, 0), (((1,), (1,)), ((), ())), preferred_element_type=F32
        )
        total[...] += image * image
        return carry

    lax.fori_loop(0, count // group, one_group, 0, unroll=min(count // group, 2))
    folded = total[:, :padded]
    for block in range(1, 2 * group):
        folded = folded + total[:, block * padded : (block + 1) * padded]
    out[0] = folded.T[: out.shape[1]] * (4.0 / count)


def swapped(values, peers, step):
    return lax.ppermute(values, "mod", [(i, i ^ step) for i in range(peers)])


def shards(screens, footprint, fraction, tilt_steps, facet_shift):
    peers = lax.axis_size("mod")
    layers, band, width = screens.shape
    count = tilt_steps.shape[0] * peers
    group = math.gcd(count, 4)
    rows = PAD // peers
    padded = round_up(rows, 16)
    lanes = round_up(P_SIZE + count + 1, 128)
    hbm = pl.BlockSpec(memory_space=pltpu.HBM)
    vmem = pl.BlockSpec(memory_space=pltpu.VMEM)
    params = pltpu.CompilerParams(vmem_limit_bytes=40 * 1024 * 1024)
    half_shape = jax.ShapeDtypeStruct((HALF, lanes), I16)
    keep, send = pl.pallas_call(
        functools.partial(phase_kernel, lanes=lanes),
        out_shape=(half_shape, half_shape),
        in_specs=[hbm, hbm, hbm, hbm],
        out_specs=(vmem, vmem),
        scratch_shapes=[
            pltpu.SMEM((1, 2, layers), I32),
            pltpu.SMEM((1, 2, layers), I32),
            pltpu.SMEM(tilt_steps.shape, I32),
            pltpu.VMEM(screens.shape, F32),
            pltpu.SemaphoreType.DMA((3,)),
            pltpu.SemaphoreType.DMA((layers,)),
        ],
        compiler_params=pltpu.CompilerParams(vmem_limit_bytes=60 * 1024 * 1024),
        name="phase_parts",
    )(footprint.swapaxes(1, 2), fraction.swapaxes(1, 2), tilt_steps, screens)
    own = keep + swapped(send, peers, 1)
    left, right, turns, passed = pl.pallas_call(
        functools.partial(table_kernel, rows=rows, padded=padded, lanes=lanes),
        out_shape=(
            jax.ShapeDtypeStruct((4 * padded, P_SIZE), BF16),
            jax.ShapeDtypeStruct((PAD, 4 * P_SIZE), BF16),
            jax.ShapeDtypeStruct((8, lanes), I32),
            half_shape,
        ),
        in_specs=[hbm, vmem],
        out_specs=(vmem, vmem, vmem, vmem),
        scratch_shapes=[pltpu.SMEM((2, 4), I32), pltpu.SemaphoreType.DMA(())],
        compiler_params=params,
        cost_estimate=pl.CostEstimate(flops=5_000_000_000, bytes_accessed=20_000_000, transcendentals=0),
        name="half_band_tables",
    )(facet_shift.T, own)
    step = 2
    while step < peers:
        own = passed = passed + swapped(own, peers, step)
        step *= 2
    other = swapped(own, peers, 1)
    return pl.pallas_call(
        functools.partial(image_kernel, count=count, group=group, padded=padded, lanes=lanes),
        out_shape=jax.ShapeDtypeStruct((1, rows, PAD), F32),
        in_specs=[vmem, vmem, vmem, vmem, vmem],
        out_specs=vmem,
        scratch_shapes=[
            pltpu.VMEM((count, P_SIZE, 128), F32),
            pltpu.VMEM((count, P_SIZE, 128), F32),
            pltpu.VMEM((count, 8, lanes), F32),
            pltpu.VMEM((count, 8, lanes), F32),
            pltpu.VMEM((P_SIZE, lanes), F32),
            pltpu.VMEM((P_SIZE, lanes), F32),
            pltpu.VMEM((PAD, 2 * group * padded), F32),
        ],
        compiler_params=params,
        name="detector_rows",
    )(turns, own, other, left, right)


def solution(mesh):
    placed = (
        P("group", "mod", None),
        P(("group", "dir"), None, None),
        P(("group", "dir"), None, None),
        P(("group", "mod"), None),
        P(),
    )
    return jax.shard_map(
        shards,
        mesh=mesh,
        in_specs=placed,
        out_specs=P(("group", "dir"), "mod", None),
        check_vma=False,
    )
```

```python
import functools
import math

import jax
import jax.numpy as jnp
from jax import lax
from jax.experimental import pallas as pl
from jax.experimental.pallas import tpu as pltpu
from jax.sharding import PartitionSpec as P

P_SIZE = 320
PAD = 640
HALF = P_SIZE // 2
FINE = 8 * PAD
CENTRE = 2 * (PAD - 2)
F32 = jnp.float32
BF16 = jnp.bfloat16
I32 = jnp.int32
I16 = jnp.int16
SIN_TERMS = (6.283184916, -41.34158923, 81.59994333, -76.61447253, 41.34288235, -12.47124354)
COS_TERMS = (0.9999992108, -19.73898036, 64.92865742, -85.27162153, 58.79049212, -21.07110563)


def round_up(value, step):
    return (value + step - 1) // step * step


def horner(terms, square):
    total = jnp.full_like(square, terms[-1])
    for term in terms[-2::-1]:
        total = total * square + term
    return total


def cos_sin(turns):
    square = turns * turns
    return horner(COS_TERMS, square), horner(SIN_TERMS, square) * turns


def centred(turns):
    return turns - jnp.floor(turns + 0.5)


def iota(shape, axis):
    return lax.broadcasted_iota(I32, shape, axis)


def lane_vector(values, index):
    out = jnp.zeros(index.shape, values[0].dtype)
    for place, value in enumerate(values):
        out = jnp.where(index == place, value, out)
    return out


def phase_kernel(
    foot_hbm, frac_hbm, tilt_hbm, screens_hbm, keep, send, foot, frac, tilt, screens, small_sems, layer_sems, *, lanes
):
    layers, band, width = screens.shape
    points = tilt.shape[0]
    me = lax.axis_index("mod")
    small = [
        pltpu.make_async_copy(source, target, small_sems.at[place])
        for place, (source, target) in enumerate(((foot_hbm, foot), (frac_hbm, frac), (tilt_hbm, tilt)))
    ]
    large = [
        pltpu.make_async_copy(screens_hbm.at[layer], screens.at[layer], layer_sems.at[layer])
        for layer in range(layers)
    ]
    for copy in small + large:
        copy.start()
    for copy in small:
        copy.wait()
    index = iota((1, layers * band), 1)
    layer_of = index // band
    first = lane_vector([foot[0, 0, i] for i in range(layers)], layer_of)
    part = lane_vector([frac[0, 0, i].astype(F32) * (1.0 / 16.0) for i in range(layers)], layer_of)
    offset = me * band + index - layer_of * band - first
    delta = offset - iota((P_SIZE, layers * band), 0)
    pick = jnp.where(delta == 0, 1.0 - part, jnp.where(delta == 1, part, 0.0)).astype(BF16)
    high, low = [], []
    for layer in range(layers):
        start = foot[0, 1, layer]
        part = frac[0, 1, layer].astype(F32) * (1.0 / 16.0)
        large[layer].wait()
        rows = screens[layer]
        here = pltpu.roll(rows, lax.rem(width - start, width), 1)[:, :lanes]
        after = pltpu.roll(rows, width - 1 - start, 1)[:, :lanes]
        mixed = here * (1.0 - part) + after * part
        top = mixed.astype(BF16)
        high.append(top)
        low.append((mixed - top.astype(F32)).astype(BF16))
    total = jnp.dot(pick, jnp.concatenate(high, 0), preferred_element_type=F32)
    total = total + jnp.dot(pick, jnp.concatenate(low, 0), preferred_element_type=F32)
    coded = jnp.floor(total * (65536.0 / 6.283185307179586) + 0.5).astype(I32)
    coded = lax.shift_right_arithmetic(lax.shift_left(coded, 16), 16)
    row = iota((HALF, lanes), 0)
    lane = iota((HALF, lanes), 1)
    table = jnp.zeros((HALF, lanes), I32)
    for point in range(points):
        place = me * points + point
        table = jnp.where((lane == P_SIZE + place) & (row == HALF - 1), tilt[point, 0], table)
        table = jnp.where((lane == lanes - 1) & (row == place), tilt[point, 1], table)
    upper = jnp.where(lane < P_SIZE, coded[:HALF], table)
    lower = jnp.where(lane < P_SIZE, coded[HALF:], table)
    odd = lax.rem(me, 2) == 1
    keep[...] = jnp.where(odd, lower, upper).astype(I16)
    send[...] = jnp.where(odd, upper, lower).astype(I16)


def shift_of(facet, quadrant, axis):
    side = quadrant // 2 if axis == 0 else quadrant % 2
    return facet[axis, quadrant] * (2 * side - 1), side == 0


def dirichlet(steps, flip):
    size = jnp.abs(steps)
    near = jnp.minimum(size, PAD - size)
    turns = near.astype(F32) * (0.5 / PAD)
    sine = horner(SIN_TERMS, turns * turns) * turns
    negative = ((jnp.bitwise_and(steps, 3) == 3) != (steps < 0)) != flip
    value = 1.0 / (jnp.where(negative, -float(PAD), float(PAD)) * sine)
    odd = jnp.bitwise_and(steps, 1) == 1
    return jnp.where(odd, value, jnp.where(steps == 0, 0.5, 0.0))


def toeplitz(top, flip, rows, width):
    lane = iota((8, width), 1)
    lane = jnp.where(lane >= width - rows, lane - width, lane)
    first = dirichlet(top - lane, flip)
    return pltpu.roll(jnp.concatenate([first] * (rows // 8), 0), 0, 1, stride=1, stride_axis=0)


def table_kernel(facet_hbm, own, left, right, turns, passed, facet, sem, *, rows, padded, lanes):
    copy = pltpu.make_async_copy(facet_hbm, facet, sem)
    copy.start()
    passed[...] = own[...]
    copy.wait()
    first = lax.axis_index("mod") * rows
    quad = iota((8, lanes), 0)
    facet_steps = jnp.zeros((8, lanes), I32)
    blocks = PAD // 128
    spill = P_SIZE % 128
    whole = P_SIZE // 128
    narrow = round_up(P_SIZE + padded, 128)
    wide = (2 * blocks - 1) * 128
    for quadrant in range(4):
        row_shift, row_flip = shift_of(facet, quadrant, 0)
        col_shift, col_flip = shift_of(facet, quadrant, 1)
        piece = toeplitz(first - HALF - row_shift, row_flip, padded, narrow)
        left[pl.ds(quadrant * padded, padded), :] = piece[:, :P_SIZE].astype(BF16)
        facet_steps = jnp.where(quad == quadrant, (row_shift + col_shift) * (-2 * (PAD - 2)), facet_steps)
    turns[...] = facet_steps
    lane = iota((128, 128), 1)
    for pair in range(2):
        pieces = []
        for side in range(2):
            col_shift, col_flip = shift_of(facet, 2 * pair + side, 1)
            top = (blocks - 1) * 128 + side * spill - HALF - col_shift
            pieces.append(toeplitz(top, col_flip, 128, wide))
        for block in range(blocks):
            even, odd = (piece[:, (blocks - 1 - block) * 128 :] for piece in pieces)
            edge = jnp.where(lane < spill, even[:, whole * 128 : whole * 128 + 128], odd[:, :128])
            joined = [even[:, : whole * 128], edge, odd[:, 128 : whole * 128 + 128]]
            right[pl.ds(block * 128, 128), pl.ds(pair * 2 * P_SIZE, 2 * P_SIZE)] = jnp.concatenate(joined, 1).astype(BF16)


def image_kernel(
    facet_steps, own, other, left, right, out, row_re, row_im, col_re, col_im, field_re, field_im, total, *, count, group, padded, lanes
):
    me = lax.axis_index("mod")
    odd = lax.rem(me, 2) == 1
    mine = own[...].astype(I32)
    theirs = other[...].astype(I32)
    coded = jnp.concatenate([jnp.where(odd, theirs, mine), jnp.where(odd, mine, theirs)], 0)
    wave_re, wave_im = cos_sin(coded.astype(F32) * (1.0 / 65536.0))
    along_y = 2 * iota((P_SIZE, lanes), 0) - (P_SIZE - 1)
    along_x = 2 * iota((P_SIZE, lanes), 1) - (P_SIZE - 1)
    radius = along_y * along_y + along_x * along_x
    edge = P_SIZE * 28 // 100
    inside = (radius <= P_SIZE * P_SIZE) & (radius >= edge * edge)
    field_re[...] = jnp.where(inside, wave_re, 0.0)
    field_im[...] = jnp.where(inside, wave_im, 0.0)
    base = P_SIZE // 128 * 128
    tilt_row = mine[HALF - 1 : HALF, base : base + 128]
    steps = (tilt_row - CENTRE) * iota((P_SIZE, 128), 0)
    cos_rows, sin_rows = cos_sin(centred(steps.astype(F32) * (1.0 / FINE)))
    for point in range(count):
        place = P_SIZE - base + point
        row_re[point] = jnp.broadcast_to(cos_rows[:, place : place + 1], (P_SIZE, 128))
        row_im[point] = jnp.broadcast_to(sin_rows[:, place : place + 1], (P_SIZE, 128))
    for point in range(count):
        tilt_col = mine[point : point + 1, lanes - 1 : lanes]
        steps = (tilt_col - CENTRE) * iota((8, lanes), 1) + facet_steps[...]
        turn_re, turn_im = cos_sin(centred(steps.astype(F32) * (1.0 / FINE)))
        col_re[point] = turn_re
        col_im[point] = turn_im
    total[...] = jnp.zeros_like(total)

    def one_group(index, carry):
        copies = lanes // 128
        stacked = []
        for member in range(group):
            point = index * group + member
            turn_re = jnp.concatenate([row_re[point]] * copies, 1)
            turn_im = jnp.concatenate([row_im[point]] * copies, 1)
            wide_re, wide_im = field_re[...], field_im[...]
            moved_re = (wide_re * turn_re - wide_im * turn_im).astype(BF16)
            moved_im = (wide_re * turn_im + wide_im * turn_re).astype(BF16)
            half = jnp.dot(left[...], jnp.concatenate([moved_re, moved_im], 1), preferred_element_type=F32)
            parts_re, parts_im = [], []
            for quadrant in range(4):
                piece = half[quadrant * padded : (quadrant + 1) * padded]
                piece_re, piece_im = piece[:, :lanes], piece[:, lanes:]
                turn_re = col_re[point, quadrant : quadrant + 1, :]
                turn_im = col_im[point, quadrant : quadrant + 1, :]
                parts_re.append((piece_re * turn_re - piece_im * turn_im).astype(BF16)[:, :P_SIZE])
                parts_im.append((piece_re * turn_im + piece_im * turn_re).astype(BF16)[:, :P_SIZE])
            stacked += [jnp.concatenate(parts_re, 1), jnp.concatenate(parts_im, 1)]
        image = lax.dot_general(
            right[...], jnp.concatenate(stacked, 0), (((1,), (1,)), ((), ())), preferred_element_type=F32
        )
        total[...] += image * image
        return carry

    lax.fori_loop(0, count // group, one_group, 0, unroll=min(count // group, 2))
    folded = total[:, :padded]
    for block in range(1, 2 * group):
        folded = folded + total[:, block * padded : (block + 1) * padded]
    out[0] = folded.T[: out.shape[1]] * (4.0 / count)


def swapped(values, peers, step):
    return lax.ppermute(values, "mod", [(i, i ^ step) for i in range(peers)])


def shards(screens, footprint, fraction, tilt_steps, facet_shift):
    peers = lax.axis_size("mod")
    layers, band, width = screens.shape
    count = tilt_steps.shape[0] * peers
    group = math.gcd(count, 4)
    rows = PAD // peers
    padded = round_up(rows, 16)
    lanes = round_up(P_SIZE + count + 1, 128)
    hbm = pl.BlockSpec(memory_space=pltpu.HBM)
    vmem = pl.BlockSpec(memory_space=pltpu.VMEM)
    params = pltpu.CompilerParams(vmem_limit_bytes=40 * 1024 * 1024)
    half_shape = jax.ShapeDtypeStruct((HALF, lanes), I16)
    keep, send = pl.pallas_call(
        functools.partial(phase_kernel, lanes=lanes),
        out_shape=(pltpu.VMEM((HALF, lanes), I16), pltpu.VMEM((HALF, lanes), I16)),
        in_specs=[hbm, hbm, hbm, hbm],
        out_specs=(vmem, vmem),
        scratch_shapes=[
            pltpu.SMEM((1, 2, layers), I32),
            pltpu.SMEM((1, 2, layers), I32),
            pltpu.SMEM(tilt_steps.shape, I32),
            pltpu.VMEM(screens.shape, F32),
            pltpu.SemaphoreType.DMA((3,)),
            pltpu.SemaphoreType.DMA((layers,)),
        ],
        compiler_params=pltpu.CompilerParams(vmem_limit_bytes=60 * 1024 * 1024),
        name="phase_parts",
    )(footprint.swapaxes(1, 2), fraction.swapaxes(1, 2), tilt_steps, screens)
    own = keep + swapped(send, peers, 1)
    left, right, turns, passed = pl.pallas_call(
        functools.partial(table_kernel, rows=rows, padded=padded, lanes=lanes),
        out_shape=(
            jax.ShapeDtypeStruct((4 * padded, P_SIZE), BF16),
            jax.ShapeDtypeStruct((PAD, 4 * P_SIZE), BF16),
            jax.ShapeDtypeStruct((8, lanes), I32),
            half_shape,
        ),
        in_specs=[hbm, vmem],
        out_specs=(vmem, vmem, vmem, vmem),
        scratch_shapes=[pltpu.SMEM((2, 4), I32), pltpu.SemaphoreType.DMA(())],
        compiler_params=params,
        cost_estimate=pl.CostEstimate(flops=5_000_000_000, bytes_accessed=20_000_000, transcendentals=0),
        name="half_band_tables",
    )(facet_shift.T, own)
    step = 2
    while step < peers:
        own = passed = passed + swapped(own, peers, step)
        step *= 2
    other = swapped(own, peers, 1)
    return pl.pallas_call(
        functools.partial(image_kernel, count=count, group=group, padded=padded, lanes=lanes),
        out_shape=jax.ShapeDtypeStruct((1, rows, PAD), F32),
        in_specs=[vmem, vmem, vmem, vmem, vmem],
        out_specs=vmem,
        scratch_shapes=[
            pltpu.VMEM((count, P_SIZE, 128), F32),
            pltpu.VMEM((count, P_SIZE, 128), F32),
            pltpu.VMEM((count, 8, lanes), F32),
            pltpu.VMEM((count, 8, lanes), F32),
            pltpu.VMEM((P_SIZE, lanes), F32),
            pltpu.VMEM((P_SIZE, lanes), F32),
            pltpu.VMEM((PAD, 2 * group * padded), F32),
        ],
        compiler_params=params,
        name="detector_rows",
    )(turns, own, other, left, right)


def solution(mesh):
    placed = (
        P("group", "mod", None),
        P(("group", "dir"), None, None),
        P(("group", "dir"), None, None),
        P(("group", "mod"), None),
        P(),
    )
    return jax.shard_map(
        shards,
        mesh=mesh,
        in_specs=placed,
        out_specs=P(("group", "dir"), "mod", None),
        check_vma=False,
    )
```

```python
import functools
import math

import jax
import jax.numpy as jnp
from jax import lax
from jax.experimental import pallas as pl
from jax.experimental.pallas import tpu as pltpu
from jax.sharding import PartitionSpec as P

P_SIZE = 320
PAD = 640
HALF = P_SIZE // 2
FINE = 8 * PAD
CENTRE = 2 * (PAD - 2)
F32 = jnp.float32
BF16 = jnp.bfloat16
I32 = jnp.int32
I16 = jnp.int16
SIN_TERMS = (6.283184916, -41.34158923, 81.59994333, -76.61447253, 41.34288235, -12.47124354)
COS_TERMS = (0.9999992108, -19.73898036, 64.92865742, -85.27162153, 58.79049212, -21.07110563)


def round_up(value, step):
    return (value + step - 1) // step * step


def horner(terms, square):
    total = jnp.full_like(square, terms[-1])
    for term in terms[-2::-1]:
        total = total * square + term
    return total


def cos_sin(turns):
    square = turns * turns
    return horner(COS_TERMS, square), horner(SIN_TERMS, square) * turns


def centred(turns):
    return turns - jnp.floor(turns + 0.5)


def iota(shape, axis):
    return lax.broadcasted_iota(I32, shape, axis)


def lane_vector(values, index):
    out = jnp.zeros(index.shape, values[0].dtype)
    for place, value in enumerate(values):
        out = jnp.where(index == place, value, out)
    return out


def phase_kernel(
    foot_hbm, frac_hbm, tilt_hbm, screens_hbm, keep, send, foot, frac, tilt, screens, small_sems, layer_sems, *, lanes
):
    layers, band, width = screens.shape
    points = tilt.shape[0]
    me = lax.axis_index("mod")
    small = [
        pltpu.make_async_copy(source, target, small_sems.at[place])
        for place, (source, target) in enumerate(((foot_hbm, foot), (frac_hbm, frac), (tilt_hbm, tilt)))
    ]
    large = [
        pltpu.make_async_copy(screens_hbm.at[layer], screens.at[layer], layer_sems.at[layer])
        for layer in range(layers)
    ]
    for copy in small + large:
        copy.start()
    for copy in small:
        copy.wait()
    index = iota((1, layers * band), 1)
    layer_of = index // band
    first = lane_vector([foot[0, 0, i] for i in range(layers)], layer_of)
    part = lane_vector([frac[0, 0, i].astype(F32) * (1.0 / 16.0) for i in range(layers)], layer_of)
    offset = me * band + index - layer_of * band - first
    delta = offset - iota((P_SIZE, layers * band), 0)
    pick = jnp.where(delta == 0, 1.0 - part, jnp.where(delta == 1, part, 0.0)).astype(BF16)
    high, low = [], []
    for layer in range(layers):
        start = foot[0, 1, layer]
        part = frac[0, 1, layer].astype(F32) * (1.0 / 16.0)
        large[layer].wait()
        rows = screens[layer]
        here = pltpu.roll(rows, lax.rem(width - start, width), 1)[:, :lanes]
        after = pltpu.roll(rows, width - 1 - start, 1)[:, :lanes]
        mixed = here * (1.0 - part) + after * part
        top = mixed.astype(BF16)
        high.append(top)
        low.append((mixed - top.astype(F32)).astype(BF16))
    total = jnp.dot(pick, jnp.concatenate(high, 0), preferred_element_type=F32)
    total = total + jnp.dot(pick, jnp.concatenate(low, 0), preferred_element_type=F32)
    coded = jnp.floor(total * (65536.0 / 6.283185307179586) + 0.5).astype(I32)
    coded = lax.shift_right_arithmetic(lax.shift_left(coded, 16), 16)
    row = iota((HALF, lanes), 0)
    lane = iota((HALF, lanes), 1)
    table = jnp.zeros((HALF, lanes), I32)
    for point in range(points):
        place = me * points + point
        table = jnp.where((lane == P_SIZE + place) & (row == HALF - 1), tilt[point, 0], table)
        table = jnp.where((lane == lanes - 1) & (row == place), tilt[point, 1], table)
    upper = jnp.where(lane < P_SIZE, coded[:HALF], table)
    lower = jnp.where(lane < P_SIZE, coded[HALF:], table)
    odd = lax.rem(me, 2) == 1
    keep[...] = jnp.where(odd, lower, upper).astype(I16)
    send[...] = jnp.where(odd, upper, lower).astype(I16)


def shift_of(facet, quadrant, axis):
    side = quadrant // 2 if axis == 0 else quadrant % 2
    return facet[axis, quadrant] * (2 * side - 1), side == 0


def dirichlet(steps, flip):
    size = jnp.abs(steps)
    near = jnp.minimum(size, PAD - size)
    turns = near.astype(F32) * (0.5 / PAD)
    sine = horner(SIN_TERMS, turns * turns) * turns
    negative = ((jnp.bitwise_and(steps, 3) == 3) != (steps < 0)) != flip
    value = 1.0 / (jnp.where(negative, -float(PAD), float(PAD)) * sine)
    odd = jnp.bitwise_and(steps, 1) == 1
    return jnp.where(odd, value, jnp.where(steps == 0, 0.5, 0.0))


def toeplitz(top, flip, rows, width):
    lane = iota((8, width), 1)
    lane = jnp.where(lane >= width - rows, lane - width, lane)
    first = dirichlet(top - lane, flip)
    return pltpu.roll(jnp.concatenate([first] * (rows // 8), 0), 0, 1, stride=1, stride_axis=0)


def table_kernel(facet_hbm, own, left, right, turns, passed, facet, sem, *, rows, padded, lanes):
    copy = pltpu.make_async_copy(facet_hbm, facet, sem)
    copy.start()
    passed[...] = own[...]
    copy.wait()
    first = lax.axis_index("mod") * rows
    quad = iota((8, lanes), 0)
    facet_steps = jnp.zeros((8, lanes), I32)
    blocks = PAD // 128
    spill = P_SIZE % 128
    whole = P_SIZE // 128
    narrow = round_up(P_SIZE + padded, 128)
    wide = (2 * blocks - 1) * 128
    for quadrant in range(4):
        row_shift, row_flip = shift_of(facet, quadrant, 0)
        col_shift, col_flip = shift_of(facet, quadrant, 1)
        piece = toeplitz(first - HALF - row_shift, row_flip, padded, narrow)
        left[pl.ds(quadrant * padded, padded), :] = piece[:, :P_SIZE].astype(BF16)
        facet_steps = jnp.where(quad == quadrant, (row_shift + col_shift) * (-2 * (PAD - 2)), facet_steps)
    turns[...] = facet_steps
    lane = iota((128, 128), 1)
    for pair in range(2):
        pieces = []
        for side in range(2):
            col_shift, col_flip = shift_of(facet, 2 * pair + side, 1)
            top = (blocks - 1) * 128 + side * spill - HALF - col_shift
            pieces.append(toeplitz(top, col_flip, 128, wide))
        for block in range(blocks):
            even, odd = (piece[:, (blocks - 1 - block) * 128 :] for piece in pieces)
            edge = jnp.where(lane < spill, even[:, whole * 128 : whole * 128 + 128], odd[:, :128])
            joined = [even[:, : whole * 128], edge, odd[:, 128 : whole * 128 + 128]]
            right[pl.ds(block * 128, 128), pl.ds(pair * 2 * P_SIZE, 2 * P_SIZE)] = jnp.concatenate(joined, 1).astype(BF16)


def image_kernel(
    facet_steps, own, other, left, right, out, row_re, row_im, col_re, col_im, field_re, field_im, stack, total,
    *, count, step_pairs, padded, lanes
):
    me = lax.axis_index("mod")
    double = 2 * P_SIZE
    odd = lax.rem(me, 2) == 1
    mine = own[...].astype(I32)
    theirs = other[...].astype(I32)
    coded = jnp.concatenate([jnp.where(odd, theirs, mine), jnp.where(odd, mine, theirs)], 0)
    wave_re, wave_im = cos_sin(coded.astype(F32) * (1.0 / 65536.0))
    along_y = 2 * iota((P_SIZE, lanes), 0) - (P_SIZE - 1)
    along_x = 2 * iota((P_SIZE, lanes), 1) - (P_SIZE - 1)
    radius = along_y * along_y + along_x * along_x
    edge = P_SIZE * 28 // 100
    inside = (radius <= P_SIZE * P_SIZE) & (radius >= edge * edge)
    for target, wave in ((field_re, wave_re), (field_im, wave_im)):
        kept = jnp.where(inside, wave, 0.0)[:, :P_SIZE]
        target[...] = jnp.concatenate([kept, kept], 1)
    base = P_SIZE // 128 * 128
    tilt_row = mine[HALF - 1 : HALF, base : base + 128]
    steps = (tilt_row - CENTRE) * iota((P_SIZE, 128), 0)
    turned = cos_sin(centred(steps.astype(F32) * (1.0 / FINE)))
    lane = iota((P_SIZE, 128), 1)
    for pair in range(count // 2):
        place = P_SIZE - base + 2 * pair
        for target, wave in zip((row_re, row_im), turned):
            one = jnp.broadcast_to(wave[:, place : place + 1], (P_SIZE, 128))
            two = jnp.broadcast_to(wave[:, place + 1 : place + 2], (P_SIZE, 128))
            target[pair] = jnp.concatenate([one, jnp.where(lane < P_SIZE - base, one, two), two], 1)
        parts = []
        for point in (2 * pair, 2 * pair + 1):
            tilt_col = mine[point : point + 1, lanes - 1 : lanes]
            steps = (tilt_col - CENTRE) * iota((8, lanes), 1) + facet_steps[...]
            parts.append(cos_sin(centred(steps.astype(F32) * (1.0 / FINE))))
        for target, one, two in zip((col_re, col_im), *parts):
            target[pair] = jnp.concatenate([one[:, :P_SIZE], two[:, :P_SIZE]], 1)
    rows = 2 * padded
    period = total.shape[1] // 128
    steps = count // (2 * step_pairs)
    total[...] = jnp.zeros_like(total)

    def row_product(pair):
        turns = []
        for source in (row_re, row_im):
            one, mix, two = (source[pair, :, tile * 128 : tile * 128 + 128] for tile in range(3))
            turns.append(jnp.concatenate([one] * (base // 128) + [mix] + [two] * (base // 128), 1))
        turn_re, turn_im = turns
        wide_re, wide_im = field_re[...], field_im[...]
        moved_re = (wide_re * turn_re - wide_im * turn_im).astype(BF16)
        moved_im = (wide_re * turn_im + wide_im * turn_re).astype(BF16)
        return jnp.dot(left[...], jnp.concatenate([moved_re, moved_im], 1), preferred_element_type=F32)

    def turned_pieces(pair, product, quadrant):
        turn_re = col_re[pair, quadrant : quadrant + 1, :]
        turn_im = col_im[pair, quadrant : quadrant + 1, :]
        piece = product[quadrant * padded : (quadrant + 1) * padded]
        piece_re, piece_im = piece[:, :double], piece[:, double:]
        return (
            (piece_re * turn_re - piece_im * turn_im).astype(BF16),
            (piece_re * turn_im + piece_im * turn_re).astype(BF16),
        )

    def keep_rows(place, pieces):
        for member in range(2):
            span = slice(member * P_SIZE, (member + 1) * P_SIZE)
            for part in range(2):
                start = (2 * place + member) * rows + part * padded
                stack[start : start + padded, :] = jnp.concatenate([piece[part][:, span] for piece in pieces], 1)

    def image_chunk(start, stop):
        image = lax.dot_general(right[...], stack[start:stop, :], (((1,), (1,)), ((), ())), preferred_element_type=F32)
        for tile in range((stop - start) // 128):
            part = image[:, tile * 128 : tile * 128 + 128]
            target = (start // 128 + tile) % period * 128
            total[:, target : target + 128] += part * part

    def one_step(index, carry):
        chunks = [(start, min(start + 256, 2 * step_pairs * rows)) for start in range(0, 2 * step_pairs * rows, 256)]
        for place in range(step_pairs):
            pair = index * step_pairs + place
            ready = [chunk for chunk in chunks if chunk[1] <= 2 * place * rows]
            chunks = chunks[len(ready) :]
            product = row_product(pair)
            pieces = []
            for quadrant in range(4):
                if ready:
                    image_chunk(*ready.pop(0))
                pieces.append(turned_pieces(pair, product, quadrant))
            for chunk in ready:
                image_chunk(*chunk)
            keep_rows(place, pieces)
        for chunk in chunks:
            image_chunk(*chunk)
        return carry

    lax.fori_loop(0, steps, one_step, 0)
    folded = total[:, :padded]
    for block in range(1, period * 128 // padded):
        folded = folded + total[:, block * padded : (block + 1) * padded]
    out[0] = folded.T[: out.shape[1]] * (4.0 / count)


def swapped(values, peers, step):
    return lax.ppermute(values, "mod", [(i, i ^ step) for i in range(peers)])


def shards(screens, footprint, fraction, tilt_steps, facet_shift):
    peers = lax.axis_size("mod")
    layers, band, width = screens.shape
    count = tilt_steps.shape[0] * peers
    step_pairs = math.gcd(count // 2, 4)
    rows = PAD // peers
    padded = round_up(rows, 16)
    lanes = round_up(P_SIZE + count + 1, 128)
    hbm = pl.BlockSpec(memory_space=pltpu.HBM)
    vmem = pl.BlockSpec(memory_space=pltpu.VMEM)
    params = pltpu.CompilerParams(vmem_limit_bytes=40 * 1024 * 1024)
    half_shape = jax.ShapeDtypeStruct((HALF, lanes), I16)
    keep, send = pl.pallas_call(
        functools.partial(phase_kernel, lanes=lanes),
        out_shape=(pltpu.VMEM((HALF, lanes), I16), pltpu.VMEM((HALF, lanes), I16)),
        in_specs=[hbm, hbm, hbm, hbm],
        out_specs=(vmem, vmem),
        scratch_shapes=[
            pltpu.SMEM((1, 2, layers), I32),
            pltpu.SMEM((1, 2, layers), I32),
            pltpu.SMEM(tilt_steps.shape, I32),
            pltpu.VMEM(screens.shape, F32),
            pltpu.SemaphoreType.DMA((3,)),
            pltpu.SemaphoreType.DMA((layers,)),
        ],
        compiler_params=pltpu.CompilerParams(vmem_limit_bytes=60 * 1024 * 1024),
        name="phase_parts",
    )(footprint.swapaxes(1, 2), fraction.swapaxes(1, 2), tilt_steps, screens)
    own = keep + swapped(send, peers, 1)
    left, right, turns, passed = pl.pallas_call(
        functools.partial(table_kernel, rows=rows, padded=padded, lanes=lanes),
        out_shape=(
            jax.ShapeDtypeStruct((4 * padded, P_SIZE), BF16),
            jax.ShapeDtypeStruct((PAD, 4 * P_SIZE), BF16),
            jax.ShapeDtypeStruct((8, lanes), I32),
            half_shape,
        ),
        in_specs=[hbm, vmem],
        out_specs=(vmem, vmem, vmem, vmem),
        scratch_shapes=[pltpu.SMEM((2, 4), I32), pltpu.SemaphoreType.DMA(())],
        compiler_params=params,
        cost_estimate=pl.CostEstimate(flops=5_000_000_000, bytes_accessed=20_000_000, transcendentals=0),
        name="half_band_tables",
    )(facet_shift.T, own)
    step = 2
    while step < peers:
        own = passed = passed + swapped(own, peers, step)
        step *= 2
    other = swapped(own, peers, 1)
    return pl.pallas_call(
        functools.partial(image_kernel, count=count, step_pairs=step_pairs, padded=padded, lanes=lanes),
        out_shape=jax.ShapeDtypeStruct((1, rows, PAD), F32),
        in_specs=[vmem, vmem, vmem, vmem, vmem],
        out_specs=vmem,
        scratch_shapes=[
            pltpu.VMEM((count // 2, P_SIZE, 384), F32),
            pltpu.VMEM((count // 2, P_SIZE, 384), F32),
            pltpu.VMEM((count // 2, 8, 2 * P_SIZE), F32),
            pltpu.VMEM((count // 2, 8, 2 * P_SIZE), F32),
            pltpu.VMEM((P_SIZE, 2 * P_SIZE), F32),
            pltpu.VMEM((P_SIZE, 2 * P_SIZE), F32),
            pltpu.VMEM((4 * step_pairs * padded, 4 * P_SIZE), BF16),
            pltpu.VMEM((PAD, math.lcm(padded, 128)), F32),
        ],
        compiler_params=params,
        name="detector_rows",
    )(turns, own, other, left, right)


def solution(mesh):
    placed = (
        P("group", "mod", None),
        P(("group", "dir"), None, None),
        P(("group", "dir"), None, None),
        P(("group", "mod"), None),
        P(),
    )
    return jax.shard_map(
        shards,
        mesh=mesh,
        in_specs=placed,
        out_specs=P(("group", "dir"), "mod", None),
        check_vma=False,
    )
```

```python
import functools
import math

import jax
import jax.numpy as jnp
from jax import lax
from jax.experimental import pallas as pl
from jax.experimental.pallas import tpu as pltpu
from jax.sharding import PartitionSpec as P

P_SIZE = 320
PAD = 640
HALF = P_SIZE // 2
FINE = 8 * PAD
CENTRE = 2 * (PAD - 2)
F32 = jnp.float32
BF16 = jnp.bfloat16
I32 = jnp.int32
I16 = jnp.int16
SIN_TERMS = (6.283184916, -41.34158923, 81.59994333, -76.61447253, 41.34288235, -12.47124354)
COS_TERMS = (0.9999992108, -19.73898036, 64.92865742, -85.27162153, 58.79049212, -21.07110563)


def round_up(value, step):
    return (value + step - 1) // step * step


def horner(terms, square):
    total = jnp.full_like(square, terms[-1])
    for term in terms[-2::-1]:
        total = total * square + term
    return total


def cos_sin(turns):
    square = turns * turns
    return horner(COS_TERMS, square), horner(SIN_TERMS, square) * turns


def centred(turns):
    return turns - jnp.floor(turns + 0.5)


def iota(shape, axis):
    return lax.broadcasted_iota(I32, shape, axis)


def lane_vector(values, index):
    out = jnp.zeros(index.shape, values[0].dtype)
    for place, value in enumerate(values):
        out = jnp.where(index == place, value, out)
    return out


def phase_kernel(
    foot_hbm, frac_hbm, tilt_hbm, screens_hbm, keep, send, foot, frac, tilt, screens, small_sems, layer_sems, *, lanes
):
    layers, band, width = screens.shape
    points = tilt.shape[0]
    me = lax.axis_index("mod")
    small = [
        pltpu.make_async_copy(source, target, small_sems.at[place])
        for place, (source, target) in enumerate(((foot_hbm, foot), (frac_hbm, frac), (tilt_hbm, tilt)))
    ]
    large = [
        pltpu.make_async_copy(screens_hbm.at[layer], screens.at[layer], layer_sems.at[layer])
        for layer in range(layers)
    ]
    for copy in small + large:
        copy.start()
    for copy in small:
        copy.wait()
    index = iota((1, layers * band), 1)
    layer_of = index // band
    first = lane_vector([foot[0, 0, i] for i in range(layers)], layer_of)
    part = lane_vector([frac[0, 0, i].astype(F32) * (1.0 / 16.0) for i in range(layers)], layer_of)
    offset = me * band + index - layer_of * band - first
    delta = offset - iota((P_SIZE, layers * band), 0)
    pick = jnp.where(delta == 0, 1.0 - part, jnp.where(delta == 1, part, 0.0)).astype(BF16)
    high, low = [], []
    for layer in range(layers):
        start = foot[0, 1, layer]
        part = frac[0, 1, layer].astype(F32) * (1.0 / 16.0)
        large[layer].wait()
        rows = screens[layer]
        mixed = rows * (1.0 - part) + pltpu.roll(rows, width - 1, 1) * part
        mixed = pltpu.roll(mixed, lax.rem(width - start, width), 1)[:, :lanes]
        top = mixed.astype(BF16)
        high.append(top)
        low.append((mixed - top.astype(F32)).astype(BF16))
    both = jnp.concatenate([jnp.concatenate(high, 0), jnp.concatenate(low, 0)], 1)
    both = jnp.dot(pick, both, preferred_element_type=F32)
    total = both[:, :lanes] + both[:, lanes:]
    coded = jnp.floor(total * (65536.0 / 6.283185307179586) + 0.5).astype(I32)
    coded = lax.shift_right_arithmetic(lax.shift_left(coded, 16), 16)
    row = iota((HALF, lanes), 0)
    lane = iota((HALF, lanes), 1)
    table = jnp.zeros((HALF, lanes), I32)
    for point in range(points):
        place = me * points + point
        table = jnp.where((lane == P_SIZE + place) & (row == HALF - 1), tilt[point, 0], table)
        table = jnp.where((lane == lanes - 1) & (row == place), tilt[point, 1], table)
    upper = jnp.where(lane < P_SIZE, coded[:HALF], table)
    lower = jnp.where(lane < P_SIZE, coded[HALF:], table)
    odd = lax.rem(me, 2) == 1
    keep[...] = jnp.where(odd, lower, upper).astype(I16)
    send[...] = jnp.where(odd, upper, lower).astype(I16)


def shift_of(facet, quadrant, axis):
    side = quadrant // 2 if axis == 0 else quadrant % 2
    return facet[axis, quadrant] * (2 * side - 1), side == 0


def dirichlet(steps, flip):
    size = jnp.abs(steps)
    near = jnp.minimum(size, PAD - size)
    turns = near.astype(F32) * (0.5 / PAD)
    sine = horner(SIN_TERMS, turns * turns) * turns
    negative = ((jnp.bitwise_and(steps, 3) == 3) != (steps < 0)) != flip
    value = 1.0 / (jnp.where(negative, -float(PAD), float(PAD)) * sine)
    odd = jnp.bitwise_and(steps, 1) == 1
    return jnp.where(odd, value, jnp.where(steps == 0, 0.5, 0.0))


def toeplitz(top, flip, rows, width):
    lane = iota((8, width), 1)
    lane = jnp.where(lane >= width - rows, lane - width, lane)
    first = dirichlet(top - lane, flip)
    return pltpu.roll(jnp.concatenate([first] * (rows // 8), 0), 0, 1, stride=1, stride_axis=0)


def table_kernel(facet_hbm, own, left, right, turns, passed, facet, sem, *, rows, padded, lanes):
    copy = pltpu.make_async_copy(facet_hbm, facet, sem)
    copy.start()
    passed[...] = own[...]
    copy.wait()
    first = lax.axis_index("mod") * rows
    quad = iota((8, lanes), 0)
    facet_steps = jnp.zeros((8, lanes), I32)
    blocks = PAD // 128
    spill = P_SIZE % 128
    whole = P_SIZE // 128
    narrow = round_up(P_SIZE + padded, 128)
    wide = (2 * blocks - 1) * 128
    for quadrant in range(4):
        row_shift, row_flip = shift_of(facet, quadrant, 0)
        col_shift, col_flip = shift_of(facet, quadrant, 1)
        piece = toeplitz(first - HALF - row_shift, row_flip, padded, narrow)
        left[pl.ds(quadrant * padded, padded), :] = piece[:, :P_SIZE].astype(BF16)
        facet_steps = jnp.where(quad == quadrant, (row_shift + col_shift) * (-2 * (PAD - 2)), facet_steps)
    turns[...] = facet_steps
    lane = iota((128, 128), 1)
    for pair in range(2):
        pieces = []
        for side in range(2):
            col_shift, col_flip = shift_of(facet, 2 * pair + side, 1)
            top = (blocks - 1) * 128 + side * spill - HALF - col_shift
            pieces.append(toeplitz(top, col_flip, 128, wide))
        for block in range(blocks):
            even, odd = (piece[:, (blocks - 1 - block) * 128 :] for piece in pieces)
            edge = jnp.where(lane < spill, even[:, whole * 128 : whole * 128 + 128], odd[:, :128])
            joined = [even[:, : whole * 128], edge, odd[:, 128 : whole * 128 + 128]]
            right[pl.ds(block * 128, 128), pl.ds(pair * 2 * P_SIZE, 2 * P_SIZE)] = jnp.concatenate(joined, 1).astype(BF16)


def image_kernel(
    facet_steps, own, other, left, right, out, row_re, row_im, col_re, col_im, field_re, field_im, stack, total,
    *, count, step_pairs, padded, lanes
):
    me = lax.axis_index("mod")
    double = 2 * P_SIZE
    odd = lax.rem(me, 2) == 1
    mine = own[...].astype(I32)
    theirs = other[...].astype(I32)
    coded = jnp.concatenate([jnp.where(odd, theirs, mine), jnp.where(odd, mine, theirs)], 0)
    wave_re, wave_im = cos_sin(coded.astype(F32) * (1.0 / 65536.0))
    along_y = 2 * iota((P_SIZE, lanes), 0) - (P_SIZE - 1)
    along_x = 2 * iota((P_SIZE, lanes), 1) - (P_SIZE - 1)
    radius = along_y * along_y + along_x * along_x
    edge = P_SIZE * 28 // 100
    inside = (radius <= P_SIZE * P_SIZE) & (radius >= edge * edge)
    for target, wave in ((field_re, wave_re), (field_im, wave_im)):
        kept = jnp.where(inside, wave, 0.0)[:, :P_SIZE]
        target[...] = jnp.concatenate([kept, kept], 1)
    base = P_SIZE // 128 * 128
    tilt_row = mine[HALF - 1 : HALF, base : base + 128]
    steps = (tilt_row - CENTRE) * iota((P_SIZE, 128), 0)
    turned = cos_sin(centred(steps.astype(F32) * (1.0 / FINE)))
    lane = iota((P_SIZE, 128), 1)

    def prepare(pair):
        place = P_SIZE - base + 2 * pair
        for target, wave in zip((row_re, row_im), turned):
            one = jnp.broadcast_to(wave[:, place : place + 1], (P_SIZE, 128))
            two = jnp.broadcast_to(wave[:, place + 1 : place + 2], (P_SIZE, 128))
            target[pair] = jnp.concatenate([one, jnp.where(lane < P_SIZE - base, one, two), two], 1)
        parts = []
        for point in (2 * pair, 2 * pair + 1):
            tilt_col = mine[point : point + 1, lanes - 1 : lanes]
            steps = (tilt_col - CENTRE) * iota((8, lanes), 1) + facet_steps[...]
            parts.append(cos_sin(centred(steps.astype(F32) * (1.0 / FINE))))
        for target, one, two in zip((col_re, col_im), *parts):
            target[pair] = jnp.concatenate([one[:, :P_SIZE], two[:, :P_SIZE]], 1)

    rows = 2 * padded
    period = total.shape[1] // 128
    steps = count // (2 * step_pairs)
    total[...] = jnp.zeros_like(total)
    for pair in range(1 if steps == 1 else count // 2):
        prepare(pair)

    def row_product(pair):
        turns = []
        for source in (row_re, row_im):
            one, mix, two = (source[pair, :, tile * 128 : tile * 128 + 128] for tile in range(3))
            turns.append(jnp.concatenate([one] * (base // 128) + [mix] + [two] * (base // 128), 1))
        turn_re, turn_im = turns
        wide_re, wide_im = field_re[...], field_im[...]
        moved_re = (wide_re * turn_re - wide_im * turn_im).astype(BF16)
        moved_im = (wide_re * turn_im + wide_im * turn_re).astype(BF16)
        return jnp.dot(left[...], jnp.concatenate([moved_re, moved_im], 1), preferred_element_type=F32)

    def turned_pieces(pair, product, quadrant):
        turn_re = col_re[pair, quadrant : quadrant + 1, :]
        turn_im = col_im[pair, quadrant : quadrant + 1, :]
        piece = product[quadrant * padded : (quadrant + 1) * padded]
        piece_re, piece_im = piece[:, :double], piece[:, double:]
        return (
            (piece_re * turn_re - piece_im * turn_im).astype(BF16),
            (piece_re * turn_im + piece_im * turn_re).astype(BF16),
        )

    def keep_rows(place, pieces):
        for member in range(2):
            span = slice(member * P_SIZE, (member + 1) * P_SIZE)
            for part in range(2):
                start = (2 * place + member) * rows + part * padded
                stack[start : start + padded, :] = jnp.concatenate([piece[part][:, span] for piece in pieces], 1)

    def image_chunk(start, stop):
        image = lax.dot_general(right[...], stack[start:stop, :], (((1,), (1,)), ((), ())), preferred_element_type=F32)
        for tile in range((stop - start) // 128):
            part = image[:, tile * 128 : tile * 128 + 128]
            target = (start // 128 + tile) % period * 128
            total[:, target : target + 128] += part * part

    def one_step(index, carry):
        chunks = [(start, min(start + 256, 2 * step_pairs * rows)) for start in range(0, 2 * step_pairs * rows, 256)]
        for place in range(step_pairs):
            pair = index * step_pairs + place
            ready = [chunk for chunk in chunks if chunk[1] <= 2 * place * rows]
            chunks = chunks[len(ready) :]
            product = row_product(pair)
            pieces = []
            for quadrant in range(4):
                if ready:
                    image_chunk(*ready.pop(0))
                pieces.append(turned_pieces(pair, product, quadrant))
            for chunk in ready:
                image_chunk(*chunk)
            if steps == 1 and place + 1 < step_pairs:
                prepare(place + 1)
            keep_rows(place, pieces)
        for chunk in chunks:
            image_chunk(*chunk)
        return carry

    if steps == 1:
        one_step(0, 0)
    else:
        lax.fori_loop(0, steps, one_step, 0)
    folded = total[:, :padded]
    for block in range(1, period * 128 // padded):
        folded = folded + total[:, block * padded : (block + 1) * padded]
    out[0] = folded.T[: out.shape[1]] * (4.0 / count)


def swapped(values, peers, step):
    return lax.ppermute(values, "mod", [(i, i ^ step) for i in range(peers)])


def shards(screens, footprint, fraction, tilt_steps, facet_shift):
    peers = lax.axis_size("mod")
    layers, band, width = screens.shape
    count = tilt_steps.shape[0] * peers
    step_pairs = math.gcd(count // 2, 4)
    rows = PAD // peers
    padded = round_up(rows, 16)
    lanes = round_up(P_SIZE + count + 1, 128)
    hbm = pl.BlockSpec(memory_space=pltpu.HBM)
    vmem = pl.BlockSpec(memory_space=pltpu.VMEM)
    params = pltpu.CompilerParams(vmem_limit_bytes=40 * 1024 * 1024)
    half_shape = jax.ShapeDtypeStruct((HALF, lanes), I16)
    keep, send = pl.pallas_call(
        functools.partial(phase_kernel, lanes=lanes),
        out_shape=(pltpu.VMEM((HALF, lanes), I16), pltpu.VMEM((HALF, lanes), I16)),
        in_specs=[hbm, hbm, hbm, hbm],
        out_specs=(vmem, vmem),
        scratch_shapes=[
            pltpu.SMEM((1, 2, layers), I32),
            pltpu.SMEM((1, 2, layers), I32),
            pltpu.SMEM(tilt_steps.shape, I32),
            pltpu.VMEM(screens.shape, F32),
            pltpu.SemaphoreType.DMA((3,)),
            pltpu.SemaphoreType.DMA((layers,)),
        ],
        compiler_params=pltpu.CompilerParams(vmem_limit_bytes=60 * 1024 * 1024),
        name="phase_parts",
    )(footprint.swapaxes(1, 2), fraction.swapaxes(1, 2), tilt_steps, screens)
    own = keep + swapped(send, peers, 1)
    left, right, turns, passed = pl.pallas_call(
        functools.partial(table_kernel, rows=rows, padded=padded, lanes=lanes),
        out_shape=(
            jax.ShapeDtypeStruct((4 * padded, P_SIZE), BF16),
            jax.ShapeDtypeStruct((PAD, 4 * P_SIZE), BF16),
            jax.ShapeDtypeStruct((8, lanes), I32),
            half_shape,
        ),
        in_specs=[hbm, vmem],
        out_specs=(vmem, vmem, vmem, vmem),
        scratch_shapes=[pltpu.SMEM((2, 4), I32), pltpu.SemaphoreType.DMA(())],
        compiler_params=params,
        cost_estimate=pl.CostEstimate(flops=5_000_000_000, bytes_accessed=20_000_000, transcendentals=0),
        name="half_band_tables",
    )(facet_shift.T, own)
    step = 2
    while step < peers:
        own = passed = passed + swapped(own, peers, step)
        step *= 2
    other = swapped(own, peers, 1)
    return pl.pallas_call(
        functools.partial(image_kernel, count=count, step_pairs=step_pairs, padded=padded, lanes=lanes),
        out_shape=jax.ShapeDtypeStruct((1, rows, PAD), F32),
        in_specs=[vmem, vmem, vmem, vmem, vmem],
        out_specs=vmem,
        scratch_shapes=[
            pltpu.VMEM((count // 2, P_SIZE, 384), F32),
            pltpu.VMEM((count // 2, P_SIZE, 384), F32),
            pltpu.VMEM((count // 2, 8, 2 * P_SIZE), F32),
            pltpu.VMEM((count // 2, 8, 2 * P_SIZE), F32),
            pltpu.VMEM((P_SIZE, 2 * P_SIZE), F32),
            pltpu.VMEM((P_SIZE, 2 * P_SIZE), F32),
            pltpu.VMEM((4 * step_pairs * padded, 4 * P_SIZE), BF16),
            pltpu.VMEM((PAD, math.lcm(padded, 128)), F32),
        ],
        compiler_params=params,
        name="detector_rows",
    )(turns, own, other, left, right)


def solution(mesh):
    placed = (
        P("group", "mod", None),
        P(("group", "dir"), None, None),
        P(("group", "dir"), None, None),
        P(("group", "mod"), None),
        P(),
    )
    return jax.shard_map(
        shards,
        mesh=mesh,
        in_specs=placed,
        out_specs=P(("group", "dir"), "mod", None),
        check_vma=False,
    )
```

```python
import functools
import math

import jax
import jax.numpy as jnp
from jax import lax
from jax.experimental import pallas as pl
from jax.experimental.pallas import tpu as pltpu
from jax.sharding import PartitionSpec as P

P_SIZE = 320
PAD = 640
HALF = P_SIZE // 2
FINE = 8 * PAD
CENTRE = 2 * (PAD - 2)
F32 = jnp.float32
BF16 = jnp.bfloat16
I32 = jnp.int32
I16 = jnp.int16
SIN_TERMS = (6.283184916, -41.34158923, 81.59994333, -76.61447253, 41.34288235, -12.47124354)
COS_TERMS = (0.9999992108, -19.73898036, 64.92865742, -85.27162153, 58.79049212, -21.07110563)


def round_up(value, step):
    return (value + step - 1) // step * step


def horner(terms, square):
    total = jnp.full_like(square, terms[-1])
    for term in terms[-2::-1]:
        total = total * square + term
    return total


def cos_sin(turns):
    square = turns * turns
    return horner(COS_TERMS, square), horner(SIN_TERMS, square) * turns


def centred(turns):
    return turns - jnp.floor(turns + 0.5)


def iota(shape, axis):
    return lax.broadcasted_iota(I32, shape, axis)


def lane_vector(values, index):
    out = jnp.zeros(index.shape, values[0].dtype)
    for place, value in enumerate(values):
        out = jnp.where(index == place, value, out)
    return out


def phase_kernel(
    foot_hbm, frac_hbm, tilt_hbm, screens_hbm, keep, send, foot, frac, tilt, screens, small_sems, layer_sems, *, lanes
):
    layers, band, width = screens.shape
    points = tilt.shape[0]
    me = lax.axis_index("mod")
    small = [
        pltpu.make_async_copy(source, target, small_sems.at[place])
        for place, (source, target) in enumerate(((foot_hbm, foot), (frac_hbm, frac), (tilt_hbm, tilt)))
    ]
    large = [
        pltpu.make_async_copy(screens_hbm.at[layer], screens.at[layer], layer_sems.at[layer])
        for layer in range(layers)
    ]
    for copy in small + large:
        copy.start()
    for copy in small:
        copy.wait()
    index = iota((1, layers * band), 1)
    layer_of = index // band
    first = lane_vector([foot[0, 0, i] for i in range(layers)], layer_of)
    part = lane_vector([frac[0, 0, i].astype(F32) * (1.0 / 16.0) for i in range(layers)], layer_of)
    offset = me * band + index - layer_of * band - first
    delta = offset - iota((P_SIZE, layers * band), 0)
    pick = jnp.where(delta == 0, 1.0 - part, jnp.where(delta == 1, part, 0.0)).astype(BF16)
    high, low = [], []
    for layer in range(layers):
        start = foot[0, 1, layer]
        part = frac[0, 1, layer].astype(F32) * (1.0 / 16.0)
        large[layer].wait()
        rows = screens[layer]
        mixed = rows * (1.0 - part) + pltpu.roll(rows, width - 1, 1) * part
        mixed = pltpu.roll(mixed, lax.rem(width - start, width), 1)[:, :lanes]
        top = mixed.astype(BF16)
        high.append(top)
        low.append((mixed - top.astype(F32)).astype(BF16))
    both = jnp.concatenate([jnp.concatenate(high, 0), jnp.concatenate(low, 0)], 1)
    both = jnp.dot(pick, both, preferred_element_type=F32)
    total = both[:, :lanes] + both[:, lanes:]
    coded = jnp.floor(total * (65536.0 / 6.283185307179586) + 0.5).astype(I32)
    coded = lax.shift_right_arithmetic(lax.shift_left(coded, 16), 16)
    row = iota((HALF, lanes), 0)
    lane = iota((HALF, lanes), 1)
    table = jnp.zeros((HALF, lanes), I32)
    for point in range(points):
        place = me * points + point
        table = jnp.where((lane == P_SIZE + place) & (row == HALF - 1), tilt[point, 0], table)
        table = jnp.where((lane == lanes - 1) & (row == place), tilt[point, 1], table)
    upper = jnp.where(lane < P_SIZE, coded[:HALF], table)
    lower = jnp.where(lane < P_SIZE, coded[HALF:], table)
    odd = lax.rem(me, 2) == 1
    keep[...] = jnp.where(odd, lower, upper).astype(I16)
    send[...] = jnp.where(odd, upper, lower).astype(I16)


def shift_of(facet, quadrant, axis):
    side = quadrant // 2 if axis == 0 else quadrant % 2
    return facet[axis, quadrant] * (2 * side - 1), side == 0


def dirichlet(steps, flip):
    size = jnp.abs(steps)
    near = jnp.minimum(size, PAD - size)
    turns = near.astype(F32) * (0.5 / PAD)
    sine = horner(SIN_TERMS, turns * turns) * turns
    negative = ((jnp.bitwise_and(steps, 3) == 3) != (steps < 0)) != flip
    value = 1.0 / (jnp.where(negative, -float(PAD), float(PAD)) * sine)
    odd = jnp.bitwise_and(steps, 1) == 1
    return jnp.where(odd, value, jnp.where(steps == 0, 0.5, 0.0))


def toeplitz(top, flip, rows, width):
    lane = iota((8, width), 1)
    lane = jnp.where(lane >= width - rows, lane - width, lane)
    first = dirichlet(top - lane, flip)
    return pltpu.roll(jnp.concatenate([first] * (rows // 8), 0), 0, 1, stride=1, stride_axis=0)


def table_kernel(facet_hbm, own, left, right, turns, passed, facet, sem, *, rows, padded, lanes):
    copy = pltpu.make_async_copy(facet_hbm, facet, sem)
    copy.start()
    passed[...] = own[...]
    copy.wait()
    first = lax.axis_index("mod") * rows
    quad = iota((8, lanes), 0)
    facet_steps = jnp.zeros((8, lanes), I32)
    blocks = PAD // 128
    spill = P_SIZE % 128
    whole = P_SIZE // 128
    narrow = round_up(P_SIZE + padded, 128)
    wide = (2 * blocks - 1) * 128
    for quadrant in range(4):
        row_shift, row_flip = shift_of(facet, quadrant, 0)
        col_shift, col_flip = shift_of(facet, quadrant, 1)
        piece = toeplitz(first - HALF - row_shift, row_flip, padded, narrow)
        left[pl.ds(quadrant * padded, padded), :] = piece[:, :P_SIZE].astype(BF16)
        facet_steps = jnp.where(quad == quadrant, (row_shift + col_shift) * (-2 * (PAD - 2)), facet_steps)
    turns[...] = facet_steps
    lane = iota((128, 128), 1)
    for pair in range(2):
        pieces = []
        for side in range(2):
            col_shift, col_flip = shift_of(facet, 2 * pair + side, 1)
            top = (blocks - 1) * 128 + side * spill - HALF - col_shift
            pieces.append(toeplitz(top, col_flip, 128, wide))
        for block in range(blocks):
            even, odd = (piece[:, (blocks - 1 - block) * 128 :] for piece in pieces)
            edge = jnp.where(lane < spill, even[:, whole * 128 : whole * 128 + 128], odd[:, :128])
            joined = [even[:, : whole * 128], edge, odd[:, 128 : whole * 128 + 128]]
            right[pl.ds(block * 128, 128), pl.ds(pair * 2 * P_SIZE, 2 * P_SIZE)] = jnp.concatenate(joined, 1).astype(BF16)


def image_kernel(
    facet_steps, own, other, left, right, out, row_re, row_im, col_re, col_im, field_re, field_im, stack, total,
    *, count, step_pairs, padded, lanes
):
    me = lax.axis_index("mod")
    double = 2 * P_SIZE
    odd = lax.rem(me, 2) == 1
    mine = own[...].astype(I32)
    theirs = other[...].astype(I32)
    coded = jnp.concatenate([jnp.where(odd, theirs, mine), jnp.where(odd, mine, theirs)], 0)
    wave_re, wave_im = cos_sin(coded.astype(F32) * (1.0 / 65536.0))
    along_y = 2 * iota((P_SIZE, 1), 0) - (P_SIZE - 1)
    along_x = 2 * iota((1, lanes), 1) - (P_SIZE - 1)
    radius = along_y * along_y + along_x * along_x
    edge = P_SIZE * 28 // 100
    inside = (radius <= P_SIZE * P_SIZE) & (radius >= edge * edge)
    for target, wave in ((field_re, wave_re), (field_im, wave_im)):
        kept = jnp.where(inside, wave, 0.0)[:, :P_SIZE]
        target[...] = jnp.concatenate([kept, kept], 1)
    base = P_SIZE // 128 * 128
    tilt_row = mine[HALF - 1 : HALF, base : base + 128]
    steps = (tilt_row - CENTRE) * iota((P_SIZE, 128), 0)
    turned = cos_sin(centred(steps.astype(F32) * (1.0 / FINE)))
    lane = iota((P_SIZE, 128), 1)

    def prepare(pair):
        place = P_SIZE - base + 2 * pair
        for target, wave in zip((row_re, row_im), turned):
            one = jnp.broadcast_to(wave[:, place : place + 1], (P_SIZE, 128))
            two = jnp.broadcast_to(wave[:, place + 1 : place + 2], (P_SIZE, 128))
            target[pair] = jnp.concatenate([one, jnp.where(lane < P_SIZE - base, one, two), two], 1)
        parts = []
        for point in (2 * pair, 2 * pair + 1):
            tilt_col = mine[point : point + 1, lanes - 1 : lanes]
            steps = (tilt_col - CENTRE) * iota((8, lanes), 1) + facet_steps[...]
            parts.append(cos_sin(centred(steps.astype(F32) * (1.0 / FINE))))
        for target, one, two in zip((col_re, col_im), *parts):
            target[pair] = jnp.concatenate([one[:, :P_SIZE], two[:, :P_SIZE]], 1)

    rows = 2 * padded
    period = total.shape[1] // 128
    steps = count // (2 * step_pairs)
    total[...] = jnp.zeros_like(total)
    for pair in range(1 if steps == 1 else count // 2):
        prepare(pair)

    def row_product(pair):
        turns = []
        for source in (row_re, row_im):
            one, mix, two = (source[pair, :, tile * 128 : tile * 128 + 128] for tile in range(3))
            turns.append(jnp.concatenate([one] * (base // 128) + [mix] + [two] * (base // 128), 1))
        turn_re, turn_im = turns
        wide_re, wide_im = field_re[...], field_im[...]
        moved_re = (wide_re * turn_re - wide_im * turn_im).astype(BF16)
        moved_im = (wide_re * turn_im + wide_im * turn_re).astype(BF16)
        return jnp.dot(left[...], jnp.concatenate([moved_re, moved_im], 1), preferred_element_type=F32)

    def turned_pieces(pair, product, quadrant):
        turn_re = col_re[pair, quadrant : quadrant + 1, :]
        turn_im = col_im[pair, quadrant : quadrant + 1, :]
        piece = product[quadrant * padded : (quadrant + 1) * padded]
        piece_re, piece_im = piece[:, :double], piece[:, double:]
        return (
            (piece_re * turn_re - piece_im * turn_im).astype(BF16),
            (piece_re * turn_im + piece_im * turn_re).astype(BF16),
        )

    def keep_rows(place, pieces):
        for member in range(2):
            span = slice(member * P_SIZE, (member + 1) * P_SIZE)
            for part in range(2):
                start = (2 * place + member) * rows + part * padded
                stack[start : start + padded, :] = jnp.concatenate([piece[part][:, span] for piece in pieces], 1)

    def image_chunk(start, stop):
        image = lax.dot_general(right[...], stack[start:stop, :], (((1,), (1,)), ((), ())), preferred_element_type=F32)
        for tile in range((stop - start) // 128):
            part = image[:, tile * 128 : tile * 128 + 128]
            target = (start // 128 + tile) % period * 128
            total[:, target : target + 128] += part * part

    def one_step(index, carry):
        chunks = [(start, min(start + 256, 2 * step_pairs * rows)) for start in range(0, 2 * step_pairs * rows, 256)]
        for place in range(step_pairs):
            pair = index * step_pairs + place
            ready = [chunk for chunk in chunks if chunk[1] <= 2 * place * rows]
            chunks = chunks[len(ready) :]
            product = row_product(pair)
            pieces = []
            for quadrant in range(4):
                if ready:
                    image_chunk(*ready.pop(0))
                pieces.append(turned_pieces(pair, product, quadrant))
            if steps == 1 and place + 1 < step_pairs:
                prepare(place + 1)
            keep_rows(place, pieces)
            for chunk in ready:
                image_chunk(*chunk)
        for chunk in chunks:
            image_chunk(*chunk)
        return carry

    if steps == 1:
        one_step(0, 0)
    else:
        lax.fori_loop(0, steps, one_step, 0)
    folded = total[:, :padded]
    for block in range(1, period * 128 // padded):
        folded = folded + total[:, block * padded : (block + 1) * padded]
    out[0] = folded.T[: out.shape[1]] * (4.0 / count)


def swapped(values, peers, step):
    return lax.ppermute(values, "mod", [(i, i ^ step) for i in range(peers)])


def shards(screens, footprint, fraction, tilt_steps, facet_shift):
    peers = lax.axis_size("mod")
    layers, band, width = screens.shape
    count = tilt_steps.shape[0] * peers
    step_pairs = math.gcd(count // 2, 4)
    rows = PAD // peers
    padded = round_up(rows, 16)
    lanes = round_up(P_SIZE + count + 1, 128)
    hbm = pl.BlockSpec(memory_space=pltpu.HBM)
    vmem = pl.BlockSpec(memory_space=pltpu.VMEM)
    params = pltpu.CompilerParams(vmem_limit_bytes=40 * 1024 * 1024)
    half_shape = jax.ShapeDtypeStruct((HALF, lanes), I16)
    keep, send = pl.pallas_call(
        functools.partial(phase_kernel, lanes=lanes),
        out_shape=(pltpu.VMEM((HALF, lanes), I16), pltpu.VMEM((HALF, lanes), I16)),
        in_specs=[hbm, hbm, hbm, hbm],
        out_specs=(vmem, vmem),
        scratch_shapes=[
            pltpu.SMEM((1, 2, layers), I32),
            pltpu.SMEM((1, 2, layers), I32),
            pltpu.SMEM(tilt_steps.shape, I32),
            pltpu.VMEM(screens.shape, F32),
            pltpu.SemaphoreType.DMA((3,)),
            pltpu.SemaphoreType.DMA((layers,)),
        ],
        compiler_params=pltpu.CompilerParams(vmem_limit_bytes=60 * 1024 * 1024),
        name="phase_parts",
    )(footprint.swapaxes(1, 2), fraction.swapaxes(1, 2), tilt_steps, screens)
    own = keep + swapped(send, peers, 1)
    left, right, turns, passed = pl.pallas_call(
        functools.partial(table_kernel, rows=rows, padded=padded, lanes=lanes),
        out_shape=(
            jax.ShapeDtypeStruct((4 * padded, P_SIZE), BF16),
            jax.ShapeDtypeStruct((PAD, 4 * P_SIZE), BF16),
            jax.ShapeDtypeStruct((8, lanes), I32),
            half_shape,
        ),
        in_specs=[hbm, vmem],
        out_specs=(vmem, vmem, vmem, vmem),
        scratch_shapes=[pltpu.SMEM((2, 4), I32), pltpu.SemaphoreType.DMA(())],
        compiler_params=params,
        cost_estimate=pl.CostEstimate(flops=5_000_000_000, bytes_accessed=20_000_000, transcendentals=0),
        name="half_band_tables",
    )(facet_shift.T, own)
    step = 2
    while step < peers:
        own = passed = passed + swapped(own, peers, step)
        step *= 2
    other = swapped(own, peers, 1)
    return pl.pallas_call(
        functools.partial(image_kernel, count=count, step_pairs=step_pairs, padded=padded, lanes=lanes),
        out_shape=jax.ShapeDtypeStruct((1, rows, PAD), F32),
        in_specs=[vmem, vmem, vmem, vmem, vmem],
        out_specs=vmem,
        scratch_shapes=[
            pltpu.VMEM((count // 2, P_SIZE, 384), F32),
            pltpu.VMEM((count // 2, P_SIZE, 384), F32),
            pltpu.VMEM((count // 2, 8, 2 * P_SIZE), F32),
            pltpu.VMEM((count // 2, 8, 2 * P_SIZE), F32),
            pltpu.VMEM((P_SIZE, 2 * P_SIZE), F32),
            pltpu.VMEM((P_SIZE, 2 * P_SIZE), F32),
            pltpu.VMEM((4 * step_pairs * padded, 4 * P_SIZE), BF16),
            pltpu.VMEM((PAD, math.lcm(padded, 128)), F32),
        ],
        compiler_params=params,
        name="detector_rows",
    )(turns, own, other, left, right)


def solution(mesh):
    placed = (
        P("group", "mod", None),
        P(("group", "dir"), None, None),
        P(("group", "dir"), None, None),
        P(("group", "mod"), None),
        P(),
    )
    return jax.shard_map(
        shards,
        mesh=mesh,
        in_specs=placed,
        out_specs=P(("group", "dir"), "mod", None),
        check_vma=False,
    )
```

```python
import functools
import math

import jax
import jax.numpy as jnp
from jax import lax
from jax.experimental import pallas as pl
from jax.experimental.pallas import tpu as pltpu
from jax.sharding import PartitionSpec as P

P_SIZE = 320
PAD = 640
HALF = P_SIZE // 2
FINE = 8 * PAD
CENTRE = 2 * (PAD - 2)
F32 = jnp.float32
BF16 = jnp.bfloat16
I32 = jnp.int32
I16 = jnp.int16
SIN_TERMS = (6.283184916, -41.34158923, 81.59994333, -76.61447253, 41.34288235, -12.47124354)
COS_TERMS = (0.9999992108, -19.73898036, 64.92865742, -85.27162153, 58.79049212, -21.07110563)


def round_up(value, step):
    return (value + step - 1) // step * step


def horner(terms, square):
    total = jnp.full_like(square, terms[-1])
    for term in terms[-2::-1]:
        total = total * square + term
    return total


def cos_sin(turns):
    square = turns * turns
    return horner(COS_TERMS, square), horner(SIN_TERMS, square) * turns


def centred(turns):
    return turns - jnp.floor(turns + 0.5)


def iota(shape, axis):
    return lax.broadcasted_iota(I32, shape, axis)


def lane_vector(values, index):
    out = jnp.zeros(index.shape, values[0].dtype)
    for place, value in enumerate(values):
        out = jnp.where(index == place, value, out)
    return out


def phase_kernel(
    foot_hbm, frac_hbm, tilt_hbm, screens_hbm, keep, send, foot, frac, tilt, screens, small_sems, layer_sems, *, lanes
):
    layers, band, width = screens.shape
    points = tilt.shape[0]
    me = lax.axis_index("mod")
    small = [
        pltpu.make_async_copy(source, target, small_sems.at[place])
        for place, (source, target) in enumerate(((foot_hbm, foot), (frac_hbm, frac), (tilt_hbm, tilt)))
    ]
    large = [
        pltpu.make_async_copy(screens_hbm.at[layer], screens.at[layer], layer_sems.at[layer])
        for layer in range(layers)
    ]
    for copy in small + large:
        copy.start()
    for copy in small:
        copy.wait()
    index = iota((1, layers * band), 1)
    layer_of = index // band
    first = lane_vector([foot[0, 0, i] for i in range(layers)], layer_of)
    part = lane_vector([frac[0, 0, i].astype(F32) * (1.0 / 16.0) for i in range(layers)], layer_of)
    offset = me * band + index - layer_of * band - first
    delta = offset - iota((P_SIZE, layers * band), 0)
    pick = jnp.where(delta == 0, 1.0 - part, jnp.where(delta == 1, part, 0.0)).astype(BF16)
    high, low = [], []
    for layer in range(layers):
        start = foot[0, 1, layer]
        part = frac[0, 1, layer].astype(F32) * (1.0 / 16.0)
        large[layer].wait()
        rows = screens[layer]
        mixed = rows * (1.0 - part) + pltpu.roll(rows, width - 1, 1) * part
        mixed = pltpu.roll(mixed, lax.rem(width - start, width), 1)[:, :lanes]
        top = mixed.astype(BF16)
        high.append(top)
        low.append((mixed - top.astype(F32)).astype(BF16))
    both = jnp.concatenate([jnp.concatenate(high, 0), jnp.concatenate(low, 0)], 1)
    both = jnp.dot(pick, both, preferred_element_type=F32)
    total = both[:, :lanes] + both[:, lanes:]
    coded = jnp.floor(total * (65536.0 / 6.283185307179586) + 0.5).astype(I32)
    coded = lax.shift_right_arithmetic(lax.shift_left(coded, 16), 16)
    row = iota((HALF, lanes), 0)
    lane = iota((HALF, lanes), 1)
    table = jnp.zeros((HALF, lanes), I32)
    for point in range(points):
        place = me * points + point
        table = jnp.where((lane == P_SIZE + place) & (row == HALF - 1), tilt[point, 0], table)
        table = jnp.where((lane == lanes - 1) & (row == place), tilt[point, 1], table)
    upper = jnp.where(lane < P_SIZE, coded[:HALF], table)
    lower = jnp.where(lane < P_SIZE, coded[HALF:], table)
    odd = lax.rem(me, 2) == 1
    keep[...] = jnp.where(odd, lower, upper).astype(I16)
    send[...] = jnp.where(odd, upper, lower).astype(I16)


def shift_of(facet, quadrant, axis):
    side = quadrant // 2 if axis == 0 else quadrant % 2
    return facet[axis, quadrant] * (2 * side - 1), side == 0


def dirichlet(steps, flip):
    size = jnp.abs(steps)
    near = jnp.minimum(size, PAD - size)
    turns = near.astype(F32) * (0.5 / PAD)
    sine = horner(SIN_TERMS, turns * turns) * turns
    negative = ((jnp.bitwise_and(steps, 3) == 3) != (steps < 0)) != flip
    value = 1.0 / (jnp.where(negative, -float(PAD), float(PAD)) * sine)
    odd = jnp.bitwise_and(steps, 1) == 1
    return jnp.where(odd, value, jnp.where(steps == 0, 0.5, 0.0))


def toeplitz(top, flip, rows, width):
    lane = iota((8, width), 1)
    lane = jnp.where(lane >= width - rows, lane - width, lane)
    first = dirichlet(top - lane, flip)
    return pltpu.roll(jnp.concatenate([first] * (rows // 8), 0), 0, 1, stride=1, stride_axis=0)


def table_kernel(facet_hbm, own, left, right, turns, passed, facet, sem, *, rows, padded, lanes):
    copy = pltpu.make_async_copy(facet_hbm, facet, sem)
    copy.start()
    passed[...] = own[...]
    copy.wait()
    first = lax.axis_index("mod") * rows
    quad = iota((8, lanes), 0)
    facet_steps = jnp.zeros((8, lanes), I32)
    blocks = PAD // 128
    spill = P_SIZE % 128
    whole = P_SIZE // 128
    narrow = round_up(P_SIZE + padded, 128)
    wide = (2 * blocks - 1) * 128
    for quadrant in range(4):
        row_shift, row_flip = shift_of(facet, quadrant, 0)
        col_shift, col_flip = shift_of(facet, quadrant, 1)
        piece = toeplitz(first - HALF - row_shift, row_flip, padded, narrow)
        left[pl.ds(quadrant * padded, padded), :] = piece[:, :P_SIZE].astype(BF16)
        facet_steps = jnp.where(quad == quadrant, (row_shift + col_shift) * (-2 * (PAD - 2)), facet_steps)
    turns[...] = facet_steps
    lane = iota((128, 128), 1)
    for pair in range(2):
        pieces = []
        for side in range(2):
            col_shift, col_flip = shift_of(facet, 2 * pair + side, 1)
            top = (blocks - 1) * 128 + side * spill - HALF - col_shift
            pieces.append(toeplitz(top, col_flip, 128, wide))
        for block in range(blocks):
            even, odd = (piece[:, (blocks - 1 - block) * 128 :] for piece in pieces)
            edge = jnp.where(lane < spill, even[:, whole * 128 : whole * 128 + 128], odd[:, :128])
            joined = [even[:, : whole * 128], edge, odd[:, 128 : whole * 128 + 128]]
            right[pl.ds(block * 128, 128), pl.ds(pair * 2 * P_SIZE, 2 * P_SIZE)] = jnp.concatenate(joined, 1).astype(BF16)


def image_kernel(
    facet_steps, own, other, left, right, out, row_re, row_im, col_re, col_im, field_re, field_im, stack, total,
    *, count, step_pairs, padded, lanes
):
    me = lax.axis_index("mod")
    double = 2 * P_SIZE
    odd = lax.rem(me, 2) == 1
    mine = own[...].astype(I32)
    theirs = other[...].astype(I32)
    coded = jnp.concatenate([jnp.where(odd, theirs, mine), jnp.where(odd, mine, theirs)], 0)
    wave_re, wave_im = cos_sin(coded.astype(F32) * (1.0 / 65536.0))
    along_y = 2 * iota((P_SIZE, lanes), 0) - (P_SIZE - 1)
    along_x = 2 * iota((P_SIZE, lanes), 1) - (P_SIZE - 1)
    radius = along_y * along_y + along_x * along_x
    edge = P_SIZE * 28 // 100
    inside = (radius <= P_SIZE * P_SIZE) & (radius >= edge * edge)
    for target, wave in ((field_re, wave_re), (field_im, wave_im)):
        kept = jnp.where(inside, wave, 0.0)[:, :P_SIZE]
        target[...] = jnp.concatenate([kept, kept], 1)
    base = P_SIZE // 128 * 128
    tilt_row = mine[HALF - 1 : HALF, base : base + 128]
    steps = (tilt_row - CENTRE) * iota((P_SIZE, 128), 0)
    turned = cos_sin(centred(steps.astype(F32) * (1.0 / FINE)))
    lane = iota((P_SIZE, 128), 1)

    def prepare(pair):
        place = P_SIZE - base + 2 * pair
        for target, wave in zip((row_re, row_im), turned):
            one = jnp.broadcast_to(wave[:, place : place + 1], (P_SIZE, 128))
            two = jnp.broadcast_to(wave[:, place + 1 : place + 2], (P_SIZE, 128))
            target[pair] = jnp.concatenate([one, jnp.where(lane < P_SIZE - base, one, two), two], 1)
        parts = []
        for point in (2 * pair, 2 * pair + 1):
            tilt_col = mine[point : point + 1, lanes - 1 : lanes]
            steps = (tilt_col - CENTRE) * iota((8, lanes), 1) + facet_steps[...]
            parts.append(cos_sin(centred(steps.astype(F32) * (1.0 / FINE))))
        for target, one, two in zip((col_re, col_im), *parts):
            target[pair] = jnp.concatenate([one[:, :P_SIZE], two[:, :P_SIZE]], 1)

    rows = 2 * padded
    period = total.shape[1] // 128
    steps = count // (2 * step_pairs)
    total[...] = jnp.zeros_like(total)
    for pair in range(1 if steps == 1 else count // 2):
        prepare(pair)

    def row_product(pair):
        turns = []
        for source in (row_re, row_im):
            one, mix, two = (source[pair, :, tile * 128 : tile * 128 + 128] for tile in range(3))
            turns.append(jnp.concatenate([one] * (base // 128) + [mix] + [two] * (base // 128), 1))
        turn_re, turn_im = turns
        wide_re, wide_im = field_re[...], field_im[...]
        moved_re = (wide_re * turn_re - wide_im * turn_im).astype(BF16)
        moved_im = (wide_re * turn_im + wide_im * turn_re).astype(BF16)
        return jnp.dot(left[...], jnp.concatenate([moved_re, moved_im], 1), preferred_element_type=F32)

    def turned_pieces(pair, product, quadrant):
        turn_re = col_re[pair, quadrant : quadrant + 1, :]
        turn_im = col_im[pair, quadrant : quadrant + 1, :]
        piece = product[quadrant * padded : (quadrant + 1) * padded]
        piece_re, piece_im = piece[:, :double], piece[:, double:]
        return (
            (piece_re * turn_re - piece_im * turn_im).astype(BF16),
            (piece_re * turn_im + piece_im * turn_re).astype(BF16),
        )

    def keep_rows(place, pieces):
        for member in range(2):
            span = slice(member * P_SIZE, (member + 1) * P_SIZE)
            for part in range(2):
                start = (2 * place + member) * rows + part * padded
                stack[start : start + padded, :] = jnp.concatenate([piece[part][:, span] for piece in pieces], 1)

    def image_chunk(start, stop):
        image = lax.dot_general(right[...], stack[start:stop, :], (((1,), (1,)), ((), ())), preferred_element_type=F32)
        for tile in range((stop - start) // 128):
            part = image[:, tile * 128 : tile * 128 + 128]
            target = (start // 128 + tile) % period * 128
            total[:, target : target + 128] += part * part

    def one_step(index, carry):
        chunks = [(start, min(start + 512, 2 * step_pairs * rows)) for start in range(0, 2 * step_pairs * rows, 512)]
        for place in range(step_pairs):
            pair = index * step_pairs + place
            ready = [chunk for chunk in chunks if chunk[1] <= 2 * place * rows]
            chunks = chunks[len(ready) :]
            product = row_product(pair)
            pieces = []
            for quadrant in range(4):
                if ready:
                    image_chunk(*ready.pop(0))
                pieces.append(turned_pieces(pair, product, quadrant))
            for chunk in ready:
                image_chunk(*chunk)
            if steps == 1 and place + 1 < step_pairs:
                prepare(place + 1)
            keep_rows(place, pieces)
        for chunk in chunks:
            image_chunk(*chunk)
        return carry

    if steps == 1:
        one_step(0, 0)
    else:
        lax.fori_loop(0, steps, one_step, 0)
    folded = total[:, :padded]
    for block in range(1, period * 128 // padded):
        folded = folded + total[:, block * padded : (block + 1) * padded]
    out[0] = folded.T[: out.shape[1]] * (4.0 / count)


def swapped(values, peers, step):
    return lax.ppermute(values, "mod", [(i, i ^ step) for i in range(peers)])


def shards(screens, footprint, fraction, tilt_steps, facet_shift):
    peers = lax.axis_size("mod")
    layers, band, width = screens.shape
    count = tilt_steps.shape[0] * peers
    step_pairs = math.gcd(count // 2, 4)
    rows = PAD // peers
    padded = round_up(rows, 16)
    lanes = round_up(P_SIZE + count + 1, 128)
    hbm = pl.BlockSpec(memory_space=pltpu.HBM)
    vmem = pl.BlockSpec(memory_space=pltpu.VMEM)
    params = pltpu.CompilerParams(vmem_limit_bytes=40 * 1024 * 1024)
    half_shape = jax.ShapeDtypeStruct((HALF, lanes), I16)
    keep, send = pl.pallas_call(
        functools.partial(phase_kernel, lanes=lanes),
        out_shape=(pltpu.VMEM((HALF, lanes), I16), pltpu.VMEM((HALF, lanes), I16)),
        in_specs=[hbm, hbm, hbm, hbm],
        out_specs=(vmem, vmem),
        scratch_shapes=[
            pltpu.SMEM((1, 2, layers), I32),
            pltpu.SMEM((1, 2, layers), I32),
            pltpu.SMEM(tilt_steps.shape, I32),
            pltpu.VMEM(screens.shape, F32),
            pltpu.SemaphoreType.DMA((3,)),
            pltpu.SemaphoreType.DMA((layers,)),
        ],
        compiler_params=pltpu.CompilerParams(vmem_limit_bytes=60 * 1024 * 1024),
        name="phase_parts",
    )(footprint.swapaxes(1, 2), fraction.swapaxes(1, 2), tilt_steps, screens)
    own = keep + swapped(send, peers, 1)
    left, right, turns, passed = pl.pallas_call(
        functools.partial(table_kernel, rows=rows, padded=padded, lanes=lanes),
        out_shape=(
            jax.ShapeDtypeStruct((4 * padded, P_SIZE), BF16),
            jax.ShapeDtypeStruct((PAD, 4 * P_SIZE), BF16),
            jax.ShapeDtypeStruct((8, lanes), I32),
            half_shape,
        ),
        in_specs=[hbm, vmem],
        out_specs=(vmem, vmem, vmem, vmem),
        scratch_shapes=[pltpu.SMEM((2, 4), I32), pltpu.SemaphoreType.DMA(())],
        compiler_params=params,
        cost_estimate=pl.CostEstimate(flops=5_000_000_000, bytes_accessed=20_000_000, transcendentals=0),
        name="half_band_tables",
    )(facet_shift.T, own)
    step = 2
    while step < peers:
        own = passed = passed + swapped(own, peers, step)
        step *= 2
    other = swapped(own, peers, 1)
    return pl.pallas_call(
        functools.partial(image_kernel, count=count, step_pairs=step_pairs, padded=padded, lanes=lanes),
        out_shape=jax.ShapeDtypeStruct((1, rows, PAD), F32),
        in_specs=[vmem, vmem, vmem, vmem, vmem],
        out_specs=vmem,
        scratch_shapes=[
            pltpu.VMEM((count // 2, P_SIZE, 384), F32),
            pltpu.VMEM((count // 2, P_SIZE, 384), F32),
            pltpu.VMEM((count // 2, 8, 2 * P_SIZE), F32),
            pltpu.VMEM((count // 2, 8, 2 * P_SIZE), F32),
            pltpu.VMEM((P_SIZE, 2 * P_SIZE), F32),
            pltpu.VMEM((P_SIZE, 2 * P_SIZE), F32),
            pltpu.VMEM((4 * step_pairs * padded, 4 * P_SIZE), BF16),
            pltpu.VMEM((PAD, math.lcm(padded, 128)), F32),
        ],
        compiler_params=params,
        name="detector_rows",
    )(turns, own, other, left, right)


def solution(mesh):
    placed = (
        P("group", "mod", None),
        P(("group", "dir"), None, None),
        P(("group", "dir"), None, None),
        P(("group", "mod"), None),
        P(),
    )
    return jax.shard_map(
        shards,
        mesh=mesh,
        in_specs=placed,
        out_specs=P(("group", "dir"), "mod", None),
        check_vma=False,
    )
```
